32 devices in a mesh: grp: 4 (over x, core), sub: 8 (over z, y).
Axes of the slice: x: 2, y: 2, z: 4, core: 2. Of those that a mesh axis runs over, the one named last changes fastest.
Arguments:
- embeddings: bfloat16 [24576, 1024], P(('grp', 'sub')), may hold values from -6 to 6
- cluster_id: int32 [24576], P(('grp', 'sub')), may hold values from 0 to 3, as said below
- cluster_rank: int32 [24576], P(('grp', 'sub')), may hold values from 0 to 6143, as said below
Outputs:
- best_similarity: float32 [24576], P(('grp', 'sub'))
The draws below stay inside these ranges and needn't reach their ends.
Inputs may be any that keep to these rules, and one draw needn't show every extreme that they name: `cluster_id`: every cluster 0 to 3 holds exactly 6144 documents. `cluster_rank`: within each cluster the ranks are a permutation of 0 to 6143. The documents of one device include at most 24 of one cluster whose ranks lie in one aligned block of 384 ranks, and some device has exactly 24.
All inputs are finite; a program needn't handle non-finite values.
Results may differ from the reference program's by a relative error of at most 0.0013.
Values may be sent and summed in bfloat16 or wider, within the bound.
No kernel may reach another device: no remote copies, remote signals or barrier semaphores. Data moves between devices by JAX's collectives and lax.ppermute only.
A program may use at most 128 MiB of HBM per device.

```python
import jax
import jax.numpy as jnp
from jax import lax

D = 1024
R_DEV = 768
ROWS = 24576
CLUSTER = 6144
HALF = 384
N_GRP = 4
N_SUB = 8


def build_layout(key):
    devices_all = N_GRP * N_SUB
    targets_all = 2 * devices_all
    base = R_DEV // targets_all
    pairs_all = devices_all // 2
    keys = jax.random.split(jax.random.fold_in(key, 7), 5)
    first = jax.random.randint(keys[0], (pairs_all,), 0, targets_all)
    offset = jax.random.randint(keys[1], (pairs_all,), 1, targets_all)
    second = (first + offset) % targets_all
    amount = jax.random.randint(keys[2], (pairs_all,), 0, base + 1)
    amount = amount.at[0].set(base)
    even = jnp.arange(pairs_all, dtype=jnp.int32) * 2
    odd = even + 1
    counts = jnp.full((devices_all, targets_all), base, jnp.int32)
    counts = counts.at[even, first].add(amount).at[odd, second].add(amount)
    counts = counts.at[even, second].add(-amount).at[odd, first].add(-amount)
    labels = jnp.arange(targets_all, dtype=jnp.int32)

    def expand(row_counts, row_key):
        listed = jnp.repeat(labels, row_counts, total_repeat_length=R_DEV)
        return listed[jax.random.permutation(row_key, R_DEV)]
    device_keys = jax.random.split(keys[3], devices_all)
    flat = jax.vmap(expand)(counts, device_keys).reshape(ROWS)
    tie = jax.random.permutation(keys[4], ROWS).astype(jnp.int32)
    order = jnp.argsort(flat * ROWS + tie)
    position = jnp.zeros((ROWS,), jnp.int32).at[order].set(jnp.arange(ROWS, dtype=jnp.int32))
    slot = position - flat * HALF
    group = flat // (2 * N_SUB)
    within = flat % (2 * N_SUB)
    return (group.astype(jnp.int32), (within * HALF + slot).astype(jnp.int32))


def draw_cluster_id(key, part):
    return build_layout(key)[0]


def draw_cluster_rank(key, part):
    return build_layout(key)[1]


def block_scale(stream_key, extent, shards, low, largest):
    def one(dim, shards_of):
        draws = jax.random.uniform(jax.random.fold_in(jax.random.fold_in(stream_key, 6), dim), (shards_of,), jnp.float32, low / len(shards), largest / len(shards))
        return jnp.repeat(jnp.exp(draws), extent[dim] // shards_of).reshape((-1,) + (1,) * (len(extent) - dim - 1))

    loudness = one(*shards[0])
    for cut in shards[1:]:
        loudness = loudness * one(*cut)
    return loudness


def centred(key, dims, spread, limit, pieces=(), kind=jnp.bfloat16):
    array = jax.random.normal(key, dims, jnp.float32) * spread
    if len(pieces) > 0:
        array = block_scale(key, dims, pieces, -0.22, 0.18) * array
    return jnp.clip(array, min=-limit, max=limit).astype(kind)


def setup_inputs(seed: int = 0) -> dict:
    seeds = jax.random.split(jax.random.key(seed), 4)
    embeddings = centred(seeds[0], (ROWS, D), 1.0, 6.0, ((0, 32),))
    cluster_id = draw_cluster_id(jax.random.fold_in(seeds[3], 71), 0)
    cluster_rank = draw_cluster_rank(jax.random.fold_in(seeds[3], 71), 0)
    return dict(embeddings=embeddings, cluster_id=cluster_id, cluster_rank=cluster_rank)


def reference(embeddings, cluster_id, cluster_rank):
    wide = embeddings.astype(jnp.float32)
    scale = lax.rsqrt(lax.optimization_barrier(jnp.sum(wide * wide, axis=1, keepdims=True)) + 1e-06)
    unit = lax.optimization_barrier((wide * scale).astype(jnp.bfloat16)).astype(jnp.float32)
    order = jnp.argsort(cluster_id * CLUSTER + cluster_rank).astype(jnp.int32)
    ordered = unit[order].reshape(N_GRP, CLUSTER, D)
    block = 256
    count = CLUSTER // block

    def one_cluster(members):

        def one_block(index):
            first = (index * block).astype(jnp.int32)
            rows = lax.dynamic_slice_in_dim(members, first, block, 0)
            sims = jnp.dot(rows, members.T, precision=lax.Precision.HIGHEST, preferred_element_type=jnp.float32)
            later = first + jnp.arange(block, dtype=jnp.int32)
            mask = jnp.arange(CLUSTER, dtype=jnp.int32)[None, :] < later[:, None]
            return lax.optimization_barrier(jnp.max(jnp.where(mask, sims, jnp.float32(-1.0)), axis=1))
        return lax.map(one_block, jnp.arange(count, dtype=jnp.int32)).reshape(CLUSTER)
    sorted_best = lax.map(one_cluster, ordered).reshape(ROWS)
    return jnp.zeros((ROWS,), jnp.float32).at[order].set(sorted_best)
```

```python
import functools

import jax
import jax.numpy as jnp
from jax import lax
from jax.experimental import pallas as pl
from jax.experimental.pallas import tpu as pltpu
from jax.sharding import PartitionSpec as P

AXES = ("grp", "sub")
LANES = 128
QUERY_TILE = 256
RADIX = 128
EMPTY = 255.0
VMEM = 56 * 1024 * 1024


def ceil_to(value, unit):
    return -(-value // unit) * unit


def nt_dot(left, right):
    return lax.dot_general(
        left, right, (((1,), (1,)), ((), ())), preferred_element_type=jnp.float32
    )


def dispatch_kernel(pieces, low, cap, flagged, emb, cid, rank, *refs):
    outs, place_ref, unit, slot_ref = refs[:pieces], refs[pieces], refs[pieces + 1], refs[pieces + 2]
    rows, width = emb.shape
    wide_lanes = ceil_to(cap, LANES)
    plane = lax.axis_index("sub") // low

    @pl.loop(0, rows // 64)
    def _(i):
        at = pl.ds(pl.multiple_of(i * 64, 64), 64)
        wide = emb[at, :].astype(jnp.float32)
        scale = lax.rsqrt(jnp.sum(wide * wide, axis=1, keepdims=True) + 1e-06)
        unit[at, :] = (wide * scale).astype(jnp.bfloat16)

    piece = cid[...] ^ plane
    which = lax.broadcasted_iota(jnp.int32, (16, LANES), 0)
    upper = (
        lax.broadcasted_iota(jnp.int32, (LANES, LANES), 0)
        < lax.broadcasted_iota(jnp.int32, (LANES, LANES), 1)
    ).astype(jnp.bfloat16)
    before = jnp.zeros((16, 1), jnp.float32)
    for b in range(rows // LANES):
        lanes = slice(b * LANES, (b + 1) * LANES)
        member = piece[:, lanes] == which
        ones = member.astype(jnp.float32)
        prefix = jnp.dot(ones.astype(jnp.bfloat16), upper, preferred_element_type=jnp.float32)
        slot = jnp.sum(jnp.where(member, prefix + before, 0.0), axis=0, keepdims=True)
        slot_ref[:, lanes] = slot.astype(jnp.int32)
        before = before + jnp.sum(ones, axis=1, keepdims=True)
    slot = slot_ref[...]
    place_ref[...] = piece * cap + slot
    full = jnp.max(before, axis=0, keepdims=True) > cap - 1
    full = full.astype(jnp.float32)

    target = piece * 1024 + slot
    r = rank[...]
    digits = jnp.concatenate(
        [
            (r // RADIX).astype(jnp.float32),
            (r % RADIX).astype(jnp.float32),
            jnp.ones((1, rows), jnp.float32),
            jnp.zeros((13, rows), jnp.float32),
        ],
        axis=0,
    ).astype(jnp.bfloat16)
    for s in range(pieces):
        slots = lax.broadcasted_iota(jnp.int32, (wide_lanes, rows), 0) + s * 1024
        pick = jnp.where(slots == target, 1.0, 0.0).astype(jnp.bfloat16)
        ranks = nt_dot(digits, pick)
        filled = ranks[2:3, :] > 0.5
        high = jnp.where(filled, ranks[0:1, :], EMPTY)
        parts = [high, ranks[1:2, :]]
        if flagged:
            parts.append(jnp.broadcast_to(full, (1, LANES)))
        used = 2 * wide_lanes + (LANES if flagged else 0)
        if used < width:
            parts.append(jnp.zeros((1, width - used), jnp.float32))
        note = jnp.concatenate(parts, axis=1)
        moved = jnp.dot(pick[:cap], unit[...], preferred_element_type=jnp.float32)
        outs[s][: cap - 16, :] = moved[: cap - 16].astype(jnp.bfloat16)
        last = lax.broadcasted_iota(jnp.int32, (16, 1), 0) == 15
        outs[s][cap - 16 :, :] = jnp.where(last, note, moved[cap - 16 :]).astype(jnp.bfloat16)


def dispatch(pieces, low, cap, flagged, emb, cid, rank):
    rows, width = emb.shape
    return pl.pallas_call(
        functools.partial(dispatch_kernel, pieces, low, cap, flagged),
        out_shape=[jax.ShapeDtypeStruct((cap, width), jnp.bfloat16)] * pieces
        + [jax.ShapeDtypeStruct((1, rows), jnp.int32)],
        scratch_shapes=[
            pltpu.VMEM((rows, width), jnp.bfloat16),
            pltpu.VMEM((1, rows), jnp.int32),
        ],
        compiler_params=pltpu.CompilerParams(vmem_limit_bytes=VMEM),
        name="dispatch",
    )(emb, cid.reshape(1, rows), rank.reshape(1, rows))


def similarity_kernel(pieces, ncross, cap, flagged, chunk, *refs):
    nblocks = pieces * (4 + ncross)
    blocks, refs = refs[:nblocks], refs[nblocks:]
    out_own, out_twin, out_near, out_far = refs[:4]
    home, away, cross, home_rank, away_rank, home_key, away_key, cross_key, best, sem = refs[4:]
    span = pieces * cap
    queries = home.shape[0]
    wide_lanes = ceil_to(cap, LANES)

    copies = []
    for i, block in enumerate(blocks):
        group, p = divmod(i, pieces)
        buffer, base = (
            (home, group * span) if group < 2 else
            (away, (group - 2) * span) if group < 4 else
            (cross, (group - 4) * span)
        )
        copies.append((group, p, buffer, base + p * cap))
        pltpu.make_async_copy(block, buffer.at[pl.ds(base + p * cap, cap), :], sem.at[i]).start()

    for buffer in (home, away):
        if queries > 2 * span:
            buffer[2 * span :, :] = jnp.zeros((queries - 2 * span, buffer.shape[1]), jnp.bfloat16)

    lane = lax.broadcasted_iota(jnp.int32, (1, wide_lanes), 1)
    square = lax.broadcasted_iota(jnp.int32, (cap, wide_lanes), 0) == lax.broadcasted_iota(
        jnp.int32, (cap, wide_lanes), 1
    )
    home_ranks = jnp.zeros((8, queries), jnp.float32)
    away_ranks = jnp.zeros((8, queries), jnp.float32)
    flag = jnp.zeros((1, LANES), jnp.float32)
    for i, (group, p, buffer, base) in enumerate(copies):
        pltpu.make_async_copy(blocks[i], buffer.at[pl.ds(base, cap), :], sem.at[i]).wait()
        note = buffer[base + cap - 16 : base + cap, :].astype(jnp.float32)[15:16, :]
        ranks = note[:, :wide_lanes] * RADIX + note[:, wide_lanes : 2 * wide_lanes]
        ranks = jnp.where(lane < cap - 1, ranks, EMPTY * RADIX)
        if flagged:
            flag = jnp.maximum(flag, note[:, 2 * wide_lanes : 2 * wide_lanes + LANES])
        if group < 4:
            kept = jnp.where(lane < cap, ranks, 0.0)
            row = jnp.concatenate(
                [kept, jnp.zeros((1, queries - wide_lanes), jnp.float32)], axis=1
            )
            row = pltpu.roll(jnp.broadcast_to(row, (8, queries)), base, 1)
            if group < 2:
                home_ranks = home_ranks + row
            else:
                away_ranks = away_ranks + row
        if group in (0, 2) or group >= 4:
            keys = home_key if group == 0 else away_key if group == 2 else cross_key
            column = jnp.sum(jnp.where(square, ranks, 0.0), axis=1, keepdims=True)
            keys[base : base + cap, :] = jnp.broadcast_to(column, (cap, LANES))
    home_rank[...] = home_ranks
    away_rank[...] = away_ranks

    def sweep(rows, row_rank, key_sets):
        @pl.loop(0, queries // QUERY_TILE)
        def _(t):
            at = pl.ds(pl.multiple_of(t * QUERY_TILE, QUERY_TILE), QUERY_TILE)
            query = rows[at, :]
            limit = row_rank[0:1, at]
            top = jnp.full((8, QUERY_TILE), -1.0, jnp.float32)
            for keys, key_rank, total in key_sets:
                for first in range(0, total, chunk):
                    sims = nt_dot(keys[first : first + chunk, :], query)
                    kr = key_rank[first : first + chunk, :]
                    kr = jnp.concatenate([kr] * (QUERY_TILE // LANES), axis=1)
                    sims = jnp.where(kr < limit, sims, -1.0)
                    top = jnp.maximum(
                        top, jnp.max(sims.reshape(chunk // 8, 8, QUERY_TILE), axis=0)
                    )
            best[:, at] = top

    def emit(first, second):
        got = jnp.broadcast_to(jnp.max(best[...], axis=0, keepdims=True), (8, queries))
        shown = first.shape[1] - LANES
        for out, moved in ((first, got), (second, pltpu.roll(got, queries - span, 1))):
            out[:, :shown] = moved[:, :shown]
            out[:, shown:] = jnp.broadcast_to(flag, (8, LANES))

    sweep(
        home,
        home_rank,
        [(home, home_key, span), (away, away_key, span), (cross, cross_key, ncross * span)],
    )
    emit(out_own, out_twin)
    sweep(away, away_rank, [(cross, cross_key, ncross * span)])
    emit(out_near, out_far)


def similarity(pieces, cap, flagged, own, twin, near, far, cross):
    ncross = len(cross)
    width = own[0].shape[1]
    span = pieces * cap
    queries = ceil_to(2 * span, QUERY_TILE)
    shown = ceil_to(span, LANES) + LANES
    chunk = cap * max(j for j in range(1, pieces + 1) if pieces % j == 0 and j * cap <= 832)
    groups = [own, twin, near, far] + cross
    blocks = [block for group in groups for block in group]
    f32 = jnp.float32
    return pl.pallas_call(
        functools.partial(similarity_kernel, pieces, ncross, cap, flagged, chunk),
        out_shape=[jax.ShapeDtypeStruct((8, shown), f32)] * 4,
        in_specs=[pl.BlockSpec(memory_space=pl.ANY)] * len(blocks),
        scratch_shapes=[
            pltpu.VMEM((queries, width), jnp.bfloat16),
            pltpu.VMEM((queries, width), jnp.bfloat16),
            pltpu.VMEM((ncross * span, width), jnp.bfloat16),
            pltpu.VMEM((8, queries), f32),
            pltpu.VMEM((8, queries), f32),
            pltpu.VMEM((span, LANES), f32),
            pltpu.VMEM((span, LANES), f32),
            pltpu.VMEM((ncross * span, LANES), f32),
            pltpu.VMEM((8, queries), f32),
            pltpu.SemaphoreType.DMA((len(blocks),)),
        ],
        compiler_params=pltpu.CompilerParams(vmem_limit_bytes=VMEM),
        name="similarity",
    )(*blocks)


def collect_kernel(pieces, cap, place, *refs):
    rows, out = refs[:pieces], refs[pieces]
    where = place[...]
    lane = lax.broadcasted_iota(jnp.int32, (8, LANES), 1)
    result = jnp.zeros((8, LANES), jnp.float32)
    for first in range(0, pieces * cap, LANES):
        back = rows[min(first // cap, pieces - 1)][:, first : first + LANES]
        for s in range(first // cap + 1, pieces):
            if s * cap < first + LANES:
                back = jnp.where(lane + first >= s * cap, rows[s][:, first : first + LANES], back)
        inside = where - first
        hit = (inside >= 0) & (inside < LANES)
        taken = jnp.take_along_axis(back, jnp.where(hit, inside, 0), axis=1)
        result = jnp.where(hit, taken, result)
    out[...] = result


def collect(pieces, cap, place, rows):
    return pl.pallas_call(
        functools.partial(collect_kernel, pieces, cap),
        out_shape=jax.ShapeDtypeStruct((8, LANES), jnp.float32),
        name="collect",
    )(place, *rows)


def solution(mesh):
    ngrp, nsub = mesh.shape["grp"], mesh.shape["sub"]
    low = nsub // ngrp
    pieces = ngrp
    chips = ngrp // 2

    def send(block, target):
        route = []
        for g in range(ngrp):
            for s in range(nsub):
                chip, core, plane, small = target(g // 2, g % 2, s // low, s % low)
                route.append((g * nsub + s, (chip * 2 + core) * nsub + plane * low + small))
        return lax.ppermute(block, AXES, route)

    def to_plane(block, s):
        return send(block, lambda x, c, z, y: (x, c, z ^ s, y))

    def to_twin(block):
        return send(block, lambda x, c, z, y: (x, 1 - c, z, y))

    def to_near(block):
        return send(block, lambda x, c, z, y: (x, c, z, 1 - y))

    def to_far(block):
        return send(block, lambda x, c, z, y: (x, 1 - c, z, 1 - y))

    def to_cross(block, j):
        return send(block, lambda x, c, z, y: (x ^ j, c, z, y))

    def attempt(cap, flagged, embeddings, cluster_id, cluster_rank):
        rows = embeddings.shape[0]
        *own, place = dispatch(pieces, low, cap, flagged, embeddings, cluster_id, cluster_rank)
        own = [own[0]] + [to_plane(own[s], s) for s in range(1, pieces)]
        twin = [to_twin(block) for block in own]
        near = [to_near(block) for block in own]
        far = [to_twin(block) for block in near]
        cross = [[to_cross(block, j) for block in own] for j in range(1, chips)]
        a, b, c, d = similarity(pieces, cap, flagged, own, twin, near, far, cross)
        a = jnp.maximum(jnp.maximum(a, to_twin(b)), jnp.maximum(to_near(c), to_far(d)))
        back = [a] + [to_plane(a, s) for s in range(1, pieces)]
        where = jnp.pad(place.reshape(rows // LANES, LANES), ((0, 8 - rows // LANES), (0, 0)))
        result = collect(pieces, cap, where, back)
        return result[: rows // LANES].reshape(rows), a[0, -1]

    def body(embeddings, cluster_id, cluster_rank):
        share = embeddings.shape[0] // ngrp
        usual = ceil_to(share + 1, 16)
        most = ceil_to(2 * share + 1, 16)
        result, over = attempt(usual, True, embeddings, cluster_id, cluster_rank)

        def again():
            return attempt(most, False, embeddings, cluster_id, cluster_rank)[0]

        return lax.cond(over > 0.5, again, lambda: result)

    placed = (P(AXES, None), P(AXES), P(AXES))
    return jax.shard_map(body, mesh=mesh, in_specs=placed, out_specs=P(AXES), check_vma=False)
```

```python
import functools

import jax
import jax.numpy as jnp
from jax import lax
from jax.experimental import pallas as pl
from jax.experimental.pallas import tpu as pltpu
from jax.sharding import PartitionSpec as P

AXES = ("grp", "sub")
LANES = 128
RADIX = 128
EMPTY = 255.0
VMEM = 16 * 1024 * 1024


def ceil_to(value, unit):
    return -(-value // unit) * unit


def nt_dot(left, right):
    return lax.dot_general(
        left, right, (((1,), (1,)), ((), ())), preferred_element_type=jnp.float32
    )


def flat(ref):
    return jnp.concatenate([ref[b : b + 1, :] for b in range(ref.shape[0])], axis=1)


def dispatch_kernel(pieces, low, cap, flagged, emb, cid, rank, *refs):
    outs, place_ref, unit, slot_ref = refs[:pieces], refs[pieces], refs[pieces + 1], refs[pieces + 2]
    rows, width = emb.shape
    wide_lanes = ceil_to(cap, LANES)
    plane = lax.axis_index("sub") // low

    @pl.loop(0, rows // 64)
    def _(i):
        at = pl.ds(pl.multiple_of(i * 64, 64), 64)
        wide = emb[at, :].astype(jnp.float32)
        scale = lax.rsqrt(jnp.sum(wide * wide, axis=1, keepdims=True) + 1e-06)
        unit[at, :] = (wide * scale).astype(jnp.bfloat16)

    piece = flat(cid) ^ plane
    which = lax.broadcasted_iota(jnp.int32, (16, LANES), 0)
    upper = (
        lax.broadcasted_iota(jnp.int32, (LANES, LANES), 0)
        < lax.broadcasted_iota(jnp.int32, (LANES, LANES), 1)
    ).astype(jnp.bfloat16)
    before = jnp.zeros((16, 1), jnp.float32)
    for b in range(rows // LANES):
        lanes = slice(b * LANES, (b + 1) * LANES)
        member = piece[:, lanes] == which
        ones = member.astype(jnp.float32)
        prefix = jnp.dot(ones.astype(jnp.bfloat16), upper, preferred_element_type=jnp.float32)
        slot = jnp.sum(jnp.where(member, prefix + before, 0.0), axis=0, keepdims=True)
        slot_ref[:, lanes] = slot.astype(jnp.int32)
        before = before + jnp.sum(ones, axis=1, keepdims=True)
    slot = slot_ref[...]
    place_ref[...] = piece * wide_lanes + slot
    full = jnp.max(before, axis=0, keepdims=True) > cap - 1
    full = full.astype(jnp.float32)

    target = piece * 1024 + slot
    r = flat(rank)
    digits = jnp.concatenate(
        [
            (r // RADIX).astype(jnp.float32),
            (r % RADIX).astype(jnp.float32),
            jnp.ones((1, rows), jnp.float32),
            jnp.zeros((13, rows), jnp.float32),
        ],
        axis=0,
    ).astype(jnp.bfloat16)
    for s in range(pieces):
        slots = lax.broadcasted_iota(jnp.int32, (wide_lanes, rows), 0) + s * 1024
        pick = jnp.where(slots == target, 1.0, 0.0).astype(jnp.bfloat16)
        ranks = nt_dot(digits, pick)
        filled = ranks[2:3, :] > 0.5
        high = jnp.where(filled, ranks[0:1, :], EMPTY)
        parts = [high, ranks[1:2, :]]
        if flagged:
            parts.append(jnp.broadcast_to(full, (1, LANES)))
        used = 2 * wide_lanes + (LANES if flagged else 0)
        if used < width:
            parts.append(jnp.zeros((1, width - used), jnp.float32))
        note = jnp.concatenate(parts, axis=1)
        moved = jnp.dot(pick[:cap], unit[...], preferred_element_type=jnp.float32)
        outs[s][: cap - 16, :] = moved[: cap - 16].astype(jnp.bfloat16)
        last = lax.broadcasted_iota(jnp.int32, (16, 1), 0) == 15
        outs[s][cap - 16 :, :] = jnp.where(last, note, moved[cap - 16 :]).astype(jnp.bfloat16)


def dispatch(pieces, low, cap, flagged, emb, cid, rank):
    rows, width = emb.shape
    return pl.pallas_call(
        functools.partial(dispatch_kernel, pieces, low, cap, flagged),
        out_shape=[jax.ShapeDtypeStruct((cap, width), jnp.bfloat16)] * pieces
        + [jax.ShapeDtypeStruct((1, rows), jnp.int32)],
        scratch_shapes=[
            pltpu.VMEM((rows, width), jnp.bfloat16),
            pltpu.VMEM((1, rows), jnp.int32),
        ],
        compiler_params=pltpu.CompilerParams(vmem_limit_bytes=VMEM),
        name="dispatch",
    )(emb, cid.reshape(rows // LANES, LANES), rank.reshape(rows // LANES, LANES))


def stage_kernel(p, pieces, groups, cap, flagged, chunk, *refs):
    blocks, refs = refs[:groups], refs[groups:]
    if p:
        refs = refs[4:]
    store, keys, limits, best, refs = *refs[:4], refs[4:]
    sem = refs[-1]
    lanes_per = ceil_to(cap, LANES)
    per = groups * cap
    base = p * per

    copies = []
    for g in range(groups):
        copy = pltpu.make_async_copy(blocks[g], store.at[pl.ds(base + g * cap, cap), :], sem.at[g])
        copy.start()
        copies.append(copy)

    lane = lax.broadcasted_iota(jnp.int32, (1, lanes_per), 1)
    square = lax.broadcasted_iota(jnp.int32, (cap, lanes_per), 0) == lax.broadcasted_iota(
        jnp.int32, (cap, lanes_per), 1
    )
    flag = jnp.zeros((1, LANES), jnp.float32)
    if p == 0:
        limits[...] = jnp.zeros(limits.shape, jnp.float32)
        best[...] = jnp.full(best.shape, -1.0, jnp.float32)
    for g in range(groups):
        copies[g].wait()
        end = base + (g + 1) * cap
        note = store[end - 16 : end, :].astype(jnp.float32)[15:16, :]
        ranks = note[:, :lanes_per] * RADIX + note[:, lanes_per : 2 * lanes_per]
        ranks = jnp.where(lane < cap - 1, ranks, EMPTY * RADIX)
        if flagged:
            flag = jnp.maximum(flag, note[:, 2 * lanes_per : 2 * lanes_per + LANES])
        if g in (0, 2):
            at = (2 * p + g // 2) * lanes_per
            limits[:, at : at + lanes_per] = jnp.broadcast_to(ranks, (8, lanes_per))
        column = jnp.sum(jnp.where(square, ranks, 0.0), axis=1, keepdims=True)
        keys[end - cap : end, :] = jnp.broadcast_to(column, (cap, LANES))
    if flagged:
        at = 2 * pieces * lanes_per
        best[:, at:] = jnp.maximum(best[:, at:], jnp.broadcast_to(flag, (8, LANES)))

    @pl.loop(0, 2 * p + 1)
    def _(t):
        old = t > p
        first = jnp.where(old, t - p - 1, p)
        second = jnp.where(old, p, t)
        for group, start, total in ((0, 0, per), (2, 4 * cap, per - 4 * cap)):
            query = store[pl.ds(pl.multiple_of(first * per + group * cap, 16), lanes_per), :]
            at = pl.ds(pl.multiple_of((first * 2 + group // 2) * lanes_per, LANES), lanes_per)
            limit = limits[0:1, at]
            top = best[:, at]
            for offset in range(start, start + total, chunk):
                rows = pl.ds(pl.multiple_of(second * per + offset, 16), chunk)
                sims = nt_dot(store[rows, :], query)
                kr = jnp.concatenate([keys[rows, :]] * (lanes_per // LANES), axis=1)
                sims = jnp.where(kr < limit, sims, -1.0)
                top = jnp.maximum(top, jnp.max(sims.reshape(chunk // 8, 8, lanes_per), axis=0))
            best[:, at] = top

    if p == pieces - 1:
        for group, out in enumerate(refs[:2]):
            for s in range(pieces):
                at = (2 * s + group) * lanes_per
                row = jnp.max(best[:, at : at + lanes_per], axis=0, keepdims=True)
                out[:, s * lanes_per : (s + 1) * lanes_per] = jnp.broadcast_to(row, (8, lanes_per))
            out[:, pieces * lanes_per :] = best[:, 2 * pieces * lanes_per :]


def stage(p, pieces, cap, flagged, blocks, carried):
    groups = len(blocks)
    width = blocks[0].shape[1]
    lanes_per = ceil_to(cap, LANES)
    per = groups * cap
    f32 = jnp.float32
    chunk = 2 * cap
    kept = [
        pltpu.VMEM((pieces * per, width), jnp.bfloat16),
        pltpu.VMEM((pieces * per, LANES), f32),
        pltpu.VMEM((8, 2 * pieces * lanes_per), f32),
        pltpu.VMEM((8, 2 * pieces * lanes_per + LANES), f32),
    ]
    ends = [jax.ShapeDtypeStruct((8, pieces * lanes_per + LANES), f32)] * 2
    last = p == pieces - 1
    pairs = (2 * p + 1) * (2 * per - 4 * cap) * cap
    got = pl.pallas_call(
        functools.partial(stage_kernel, p, pieces, groups, cap, flagged, chunk),
        out_shape=kept + (ends if last else []),
        in_specs=[pl.BlockSpec(memory_space=pl.ANY)] * groups
        + [pl.BlockSpec(memory_space=pltpu.VMEM)] * len(carried),
        out_specs=[pl.BlockSpec(memory_space=pltpu.VMEM)] * (4 + 2 * last),
        scratch_shapes=[pltpu.SemaphoreType.DMA((groups,))],
        input_output_aliases={groups + i: i for i in range(len(carried))},
        cost_estimate=pl.CostEstimate(
            flops=2 * pairs * width, bytes_accessed=2 * per * width, transcendentals=0
        ),
        compiler_params=pltpu.CompilerParams(vmem_limit_bytes=VMEM),
        name="stage" + str(p),
    )(*blocks, *[pltpu.with_memory_space_constraint(x, pltpu.VMEM) for x in carried])
    return got[:4], got[4:]


def collect_kernel(pieces, per, place, *refs):
    rows, out = refs[:pieces], refs[pieces]
    where = place[...]
    result = jnp.zeros((8, LANES), jnp.float32)
    for first in range(0, pieces * per, LANES):
        back = rows[first // per][:, first : first + LANES]
        inside = where - first
        hit = (inside >= 0) & (inside < LANES)
        taken = jnp.take_along_axis(back, jnp.where(hit, inside, 0), axis=1)
        result = jnp.where(hit, taken, result)
    out[...] = result


def collect(pieces, cap, place, rows):
    return pl.pallas_call(
        functools.partial(collect_kernel, pieces, ceil_to(cap, LANES)),
        out_shape=jax.ShapeDtypeStruct((8, LANES), jnp.float32),
        name="collect",
    )(place, *rows)


def solution(mesh):
    ngrp, nsub = mesh.shape["grp"], mesh.shape["sub"]
    low = nsub // ngrp
    pieces = ngrp
    chips = ngrp // 2

    def send(block, target):
        route = []
        for g in range(ngrp):
            for s in range(nsub):
                chip, core, plane, small = target(g // 2, g % 2, s // low, s % low)
                route.append((g * nsub + s, (chip * 2 + core) * nsub + plane * low + small))
        return lax.ppermute(block, AXES, route)

    def to_plane(block, s):
        return send(block, lambda x, c, z, y: (x, c, z ^ s, y))

    def to_twin(block):
        return send(block, lambda x, c, z, y: (x, 1 - c, z, y))

    def to_near(block):
        return send(block, lambda x, c, z, y: (x, c, z, 1 - y))

    def to_cross(block, j):
        return send(block, lambda x, c, z, y: (x ^ j, c, z, y))

    def attempt(cap, flagged, embeddings, cluster_id, cluster_rank):
        rows = embeddings.shape[0]
        *own, place = dispatch(pieces, low, cap, flagged, embeddings, cluster_id, cluster_rank)
        own = [own[0]] + [to_plane(own[s], s) for s in range(1, pieces)]
        carried = []
        for p in range(pieces):
            near = to_near(own[p])
            cross = [to_cross(own[p], j) for j in range(1, chips)]
            blocks = [own[p], to_twin(own[p]), near, to_twin(near)]
            blocks += cross + [to_twin(block) for block in cross]
            carried, ends = stage(p, pieces, cap, flagged, blocks, carried)
        a = jnp.maximum(ends[0], to_near(ends[1]))
        back = [a] + [to_plane(a, s) for s in range(1, pieces)]
        where = jnp.pad(place.reshape(rows // LANES, LANES), ((0, 8 - rows // LANES), (0, 0)))
        result = collect(pieces, cap, where, back)
        return result[: rows // LANES].reshape(rows), a[0, -1]

    def body(embeddings, cluster_id, cluster_rank):
        share = embeddings.shape[0] // ngrp
        usual = ceil_to(share + 1, 16)
        most = ceil_to(2 * share + 1, 16)
        result, over = attempt(usual, True, embeddings, cluster_id, cluster_rank)

        def again():
            return attempt(most, False, embeddings, cluster_id, cluster_rank)[0]

        return lax.cond(over > 0.5, again, lambda: result)

    placed = (P(AXES, None), P(AXES), P(AXES))
    return jax.shard_map(body, mesh=mesh, in_specs=placed, out_specs=P(AXES), check_vma=False)
```

```python
import functools

import jax
import jax.numpy as jnp
from jax import lax
from jax.experimental import pallas as pl
from jax.experimental.pallas import tpu as pltpu
from jax.sharding import PartitionSpec as P

AXES = ("grp", "sub")
LANES = 128
RADIX = 128
EMPTY = 255.0
VMEM = 16 * 1024 * 1024


def ceil_to(value, unit):
    return -(-value // unit) * unit


def nt_dot(left, right):
    return lax.dot_general(
        left, right, (((1,), (1,)), ((), ())), preferred_element_type=jnp.float32
    )


def steps(pieces):
    return [p ^ (p >> 1) for p in range(pieces)]


def after(blocks, earlier):
    if not earlier:
        return blocks
    held = [pltpu.with_memory_space_constraint(x, pltpu.VMEM) for x in blocks]
    return list(pl.pallas_call(
        lambda *refs: None,
        out_shape=[pltpu.VMEM(x.shape, x.dtype) for x in blocks],
        in_specs=[pl.BlockSpec(memory_space=pltpu.VMEM)] * len(blocks)
        + [pl.BlockSpec(memory_space=pl.ANY)] * len(earlier),
        out_specs=[pl.BlockSpec(memory_space=pltpu.VMEM)] * len(blocks),
        input_output_aliases={i: i for i in range(len(blocks))},
        compiler_params=pltpu.CompilerParams(vmem_limit_bytes=VMEM),
        name="after",
    )(*held, *earlier))


def flat(ref):
    return jnp.concatenate([ref[b : b + 1, :] for b in range(ref.shape[0])], axis=1)


def dispatch_kernel(pieces, low, cap, flagged, emb, cid, rank, *refs):
    outs, place_ref, unit, slot_ref = refs[:pieces], refs[pieces], refs[pieces + 1], refs[pieces + 2]
    rows, width = emb.shape
    wide_lanes = ceil_to(cap, LANES)
    plane = lax.axis_index("sub") // low

    @pl.loop(0, rows // 64)
    def _(i):
        at = pl.ds(pl.multiple_of(i * 64, 64), 64)
        wide = emb[at, :].astype(jnp.float32)
        scale = lax.rsqrt(jnp.sum(wide * wide, axis=1, keepdims=True) + 1e-06)
        unit[at, :] = (wide * scale).astype(jnp.bfloat16)

    step = flat(cid) ^ plane
    piece = jnp.zeros(step.shape, jnp.int32)
    for p, s in enumerate(steps(pieces)):
        piece = jnp.where(step == s, p, piece)
    which = lax.broadcasted_iota(jnp.int32, (16, LANES), 0)
    upper = (
        lax.broadcasted_iota(jnp.int32, (LANES, LANES), 0)
        < lax.broadcasted_iota(jnp.int32, (LANES, LANES), 1)
    ).astype(jnp.bfloat16)
    before = jnp.zeros((16, 1), jnp.float32)
    for b in range(rows // LANES):
        lanes = slice(b * LANES, (b + 1) * LANES)
        member = piece[:, lanes] == which
        ones = member.astype(jnp.float32)
        prefix = jnp.dot(ones.astype(jnp.bfloat16), upper, preferred_element_type=jnp.float32)
        slot = jnp.sum(jnp.where(member, prefix + before, 0.0), axis=0, keepdims=True)
        slot_ref[:, lanes] = slot.astype(jnp.int32)
        before = before + jnp.sum(ones, axis=1, keepdims=True)
    slot = slot_ref[...]
    place_ref[...] = piece * wide_lanes + slot
    full = jnp.max(before, axis=0, keepdims=True) > cap - 1
    full = full.astype(jnp.float32)

    target = piece * 1024 + slot
    r = flat(rank)
    digits = jnp.concatenate(
        [
            (r // RADIX).astype(jnp.float32),
            (r % RADIX).astype(jnp.float32),
            jnp.ones((1, rows), jnp.float32),
            jnp.zeros((13, rows), jnp.float32),
        ],
        axis=0,
    ).astype(jnp.bfloat16)
    for s in range(pieces):
        slots = lax.broadcasted_iota(jnp.int32, (wide_lanes, rows), 0) + s * 1024
        pick = jnp.where(slots == target, 1.0, 0.0).astype(jnp.bfloat16)
        ranks = nt_dot(digits, pick)
        filled = ranks[2:3, :] > 0.5
        high = jnp.where(filled, ranks[0:1, :], EMPTY)
        parts = [high, ranks[1:2, :]]
        if flagged:
            parts.append(jnp.broadcast_to(full, (1, LANES)))
        used = 2 * wide_lanes + (LANES if flagged else 0)
        if used < width:
            parts.append(jnp.zeros((1, width - used), jnp.float32))
        note = jnp.concatenate(parts, axis=1)
        moved = jnp.dot(pick[:cap], unit[...], preferred_element_type=jnp.float32)
        outs[s][: cap - 16, :] = moved[: cap - 16].astype(jnp.bfloat16)
        last = lax.broadcasted_iota(jnp.int32, (16, 1), 0) == 15
        outs[s][cap - 16 :, :] = jnp.where(last, note, moved[cap - 16 :]).astype(jnp.bfloat16)


def dispatch(pieces, low, cap, flagged, emb, cid, rank):
    rows, width = emb.shape
    return pl.pallas_call(
        functools.partial(dispatch_kernel, pieces, low, cap, flagged),
        out_shape=[jax.ShapeDtypeStruct((cap, width), jnp.bfloat16)] * pieces
        + [jax.ShapeDtypeStruct((1, rows), jnp.int32)],
        scratch_shapes=[
            pltpu.VMEM((rows, width), jnp.bfloat16),
            pltpu.VMEM((1, rows), jnp.int32),
        ],
        compiler_params=pltpu.CompilerParams(vmem_limit_bytes=VMEM),
        name="dispatch",
    )(emb, cid.reshape(rows // LANES, LANES), rank.reshape(rows // LANES, LANES))


def stage_kernel(p, pieces, groups, cap, flagged, *refs):
    blocks, refs = refs[:groups], refs[groups:]
    if p:
        refs = refs[5:]
    store, keys, limits, best, cols, token, refs = *refs[:6], refs[6:]
    sem = refs[-1]
    lanes_per = ceil_to(cap, LANES)
    per = groups * cap
    base = p * per
    shared = per - 2 * cap
    token[...] = jnp.zeros(token.shape, jnp.float32)

    copies = []
    for g in range(groups):
        copy = pltpu.make_async_copy(blocks[g], store.at[pl.ds(base + g * cap, cap), :], sem.at[g])
        copy.start()
        copies.append(copy)

    lane = lax.broadcasted_iota(jnp.int32, (1, lanes_per), 1)
    square = lax.broadcasted_iota(jnp.int32, (cap, lanes_per), 0) == lax.broadcasted_iota(
        jnp.int32, (cap, lanes_per), 1
    )
    flag = jnp.zeros((1, LANES), jnp.float32)
    if p == 0:
        limits[...] = jnp.zeros(limits.shape, jnp.float32)
        best[...] = jnp.full(best.shape, -1.0, jnp.float32)
        cols[...] = jnp.full(cols.shape, -1.0, jnp.float32)
        if lanes_per > cap:
            store[pieces * per :, :] = jnp.zeros((lanes_per - cap, store.shape[1]), jnp.bfloat16)
    for g in range(groups):
        copies[g].wait()
        end = base + (g + 1) * cap
        note = store[end - 16 : end, :].astype(jnp.float32)[15:16, :]
        ranks = note[:, :lanes_per] * RADIX + note[:, lanes_per : 2 * lanes_per]
        ranks = jnp.where(lane < cap - 1, ranks, EMPTY * RADIX)
        if flagged:
            flag = jnp.maximum(flag, note[:, 2 * lanes_per : 2 * lanes_per + LANES])
        if g in (0, groups - 1):
            at = (2 * p + g // (groups - 1)) * lanes_per
            limits[:, at : at + lanes_per] = jnp.broadcast_to(ranks, (8, lanes_per))
        column = jnp.sum(jnp.where(square, ranks, 0.0), axis=1, keepdims=True)
        keys[end - cap : end, :] = jnp.broadcast_to(column, (cap, LANES))
    if flagged:
        at = 2 * pieces * lanes_per
        best[:, at:] = jnp.maximum(best[:, at:], jnp.broadcast_to(flag, (8, LANES)))

    @pl.loop(0, 2 * p + 1)
    def _(t):
        old = t > p
        first = jnp.where(old, t - p - 1, p)
        second = jnp.where(old, p, t)
        for side, group in enumerate((0, groups - 1)):
            query = store[pl.ds(pl.multiple_of(first * per + group * cap, 16), lanes_per), :]
            at = pl.ds(pl.multiple_of((first * 2 + side) * lanes_per, LANES), lanes_per)
            limit = limits[0:1, at]
            top = best[:, at]
            if side == 0:
                chunks = [(0, 2 * cap)]
                chunks += [(g * cap, 2 * cap) for g in range(2, groups - 1, 2)]
                if groups % 2:
                    chunks.append(((groups - 1) * cap, cap))
            else:
                chunks = [(g * cap, cap) for g in range(2, groups - 1)]
            for offset, chunk in chunks:
                rows = pl.ds(pl.multiple_of(second * per + offset, 16), chunk)
                sims = nt_dot(store[rows, :], query)
                kr = jnp.concatenate([keys[rows, :]] * (lanes_per // LANES), axis=1)
                earlier = kr < limit
                ahead = jnp.where(earlier, sims, -1.0)
                top = jnp.maximum(top, jnp.max(ahead.reshape(chunk // 8, 8, lanes_per), axis=0))
                if offset >= 2 * cap:
                    spot = pl.ds(pl.multiple_of(second * shared + offset - 2 * cap, 16), chunk)
                    behind = jnp.where(earlier, -1.0, sims)
                    fold = cols[spot, :]
                    for k in range(0, lanes_per, LANES):
                        fold = jnp.maximum(fold, behind[:, k : k + LANES])
                    cols[spot, :] = fold
            best[:, at] = top

    if p == pieces - 1:
        for i, out in enumerate(refs[: groups - 1]):
            for s in range(pieces):
                row = jnp.full((1, lanes_per), -1.0, jnp.float32)
                if i in (0, groups - 2):
                    at = (2 * s + i // (groups - 2)) * lanes_per
                    row = jnp.max(best[:, at : at + lanes_per], axis=0, keepdims=True)
                if i:
                    at = s * shared + (i - 1) * cap
                    column = jnp.max(cols[at : at + cap, :], axis=1, keepdims=True)
                    turned = jnp.max(jnp.where(square, column, -1.0), axis=0, keepdims=True)
                    row = jnp.maximum(row, turned)
                out[:, s * lanes_per : (s + 1) * lanes_per] = jnp.broadcast_to(row, (8, lanes_per))
            out[:, pieces * lanes_per :] = best[:, 2 * pieces * lanes_per :]


def stage(p, pieces, cap, flagged, blocks, carried):
    groups = len(blocks)
    width = blocks[0].shape[1]
    lanes_per = ceil_to(cap, LANES)
    per = groups * cap
    f32 = jnp.float32
    kept = [
        pltpu.VMEM((pieces * per + lanes_per - cap, width), jnp.bfloat16),
        pltpu.VMEM((pieces * per, LANES), f32),
        pltpu.VMEM((8, 2 * pieces * lanes_per), f32),
        pltpu.VMEM((8, 2 * pieces * lanes_per + LANES), f32),
        pltpu.VMEM((pieces * (groups - 2) * cap, LANES), f32),
        jax.ShapeDtypeStruct((8, LANES), f32),
    ]
    ends = [jax.ShapeDtypeStruct((8, pieces * lanes_per + LANES), f32)] * (groups - 1)
    if p < pieces - 1:
        ends = []
    pairs = (2 * p + 1) * (2 * groups - 3) * cap * cap
    got = pl.pallas_call(
        functools.partial(stage_kernel, p, pieces, groups, cap, flagged),
        out_shape=kept + ends,
        in_specs=[pl.BlockSpec(memory_space=pl.ANY)] * groups
        + [pl.BlockSpec(memory_space=pltpu.VMEM)] * len(carried),
        out_specs=[pl.BlockSpec(memory_space=pltpu.VMEM)] * (6 + len(ends)),
        scratch_shapes=[pltpu.SemaphoreType.DMA((groups,))],
        input_output_aliases={groups + i: i for i in range(len(carried))},
        cost_estimate=pl.CostEstimate(
            flops=2 * pairs * width, bytes_accessed=2 * per * width, transcendentals=0
        ),
        compiler_params=pltpu.CompilerParams(vmem_limit_bytes=VMEM),
        name="stage" + str(p),
    )(*blocks, *[pltpu.with_memory_space_constraint(x, pltpu.VMEM) for x in carried])
    return got[:5], got[5], got[6:]


def collect_kernel(pieces, per, place, *refs):
    rows, out = refs[:pieces], refs[pieces]
    where = place[...]
    result = jnp.zeros((8, LANES), jnp.float32)
    for first in range(0, pieces * per, LANES):
        back = rows[first // per][:, first : first + LANES]
        inside = where - first
        hit = (inside >= 0) & (inside < LANES)
        taken = jnp.take_along_axis(back, jnp.where(hit, inside, 0), axis=1)
        result = jnp.where(hit, taken, result)
    out[...] = result


def collect(pieces, cap, place, rows):
    return pl.pallas_call(
        functools.partial(collect_kernel, pieces, ceil_to(cap, LANES)),
        out_shape=jax.ShapeDtypeStruct((8, LANES), jnp.float32),
        name="collect",
    )(place, *rows)


def solution(mesh):
    ngrp, nsub = mesh.shape["grp"], mesh.shape["sub"]
    low = nsub // ngrp
    pieces = ngrp
    chips = ngrp // 2

    def send(block, target):
        route = []
        for g in range(ngrp):
            for s in range(nsub):
                chip, core, plane, small = target(g // 2, g % 2, s // low, s % low)
                route.append((g * nsub + s, (chip * 2 + core) * nsub + plane * low + small))
        return lax.ppermute(block, AXES, route)

    def to_plane(block, s):
        return send(block, lambda x, c, z, y: (x, c, z ^ s, y))

    def to_twin(block):
        return send(block, lambda x, c, z, y: (x, 1 - c, z, y))

    def bit(x, j):
        return (x // (j & -j)) % 2

    def to_near(block):
        return send(block, lambda x, c, z, y: (x, c ^ (1 - y), z, 1 - y))

    def from_near(block):
        return send(block, lambda x, c, z, y: (x, c ^ y, z, 1 - y))

    def to_cross(block, j):
        return send(block, lambda x, c, z, y: (x ^ j, c ^ y ^ bit(x ^ j, j), z, y))

    def from_cross(block, j):
        return send(block, lambda x, c, z, y: (x ^ j, c ^ y ^ bit(x, j), z, y))

    def attempt(cap, flagged, embeddings, cluster_id, cluster_rank):
        rows = embeddings.shape[0]
        *own, place = dispatch(pieces, low, cap, flagged, embeddings, cluster_id, cluster_rank)
        step = steps(pieces)
        moved = [own[0]] + [None] * (pieces - 1)
        carried, token, ends = [], None, None
        for p in range(1, pieces):
            moved[p] = to_plane(own[p], step[p])
        earlier = []
        for p in range(pieces):
            (mine,) = after([moved[p]], earlier)
            cross = [to_cross(mine, j) for j in range(1, chips)]
            near = to_near(mine)
            earlier = cross + [near]
            blocks = [mine, to_twin(mine)] + cross + [near]
            carried, token, ends = stage(p, pieces, cap, flagged, blocks, carried)
        a = jnp.maximum(ends[0], from_near(ends[-1]))
        for j in range(1, chips):
            a = jnp.maximum(a, from_cross(ends[j], j))
        back = [a] + [to_plane(a, s) for s in step[1:]]
        where = jnp.pad(place.reshape(rows // LANES, LANES), ((0, 8 - rows // LANES), (0, 0)))
        result = collect(pieces, cap, where, back)
        return result[: rows // LANES].reshape(rows), a[0, -1]

    def body(embeddings, cluster_id, cluster_rank):
        share = embeddings.shape[0] // ngrp
        usual = ceil_to(share + 1, 16)
        most = ceil_to(2 * share + 1, 16)
        result, over = attempt(usual, True, embeddings, cluster_id, cluster_rank)

        def again():
            return attempt(most, False, embeddings, cluster_id, cluster_rank)[0]

        return lax.cond(over > 0.5, again, lambda: result)

    placed = (P(AXES, None), P(AXES), P(AXES))
    return jax.shard_map(body, mesh=mesh, in_specs=placed, out_specs=P(AXES), check_vma=False)
```

```python
import functools

import jax
import jax.numpy as jnp
from jax import lax
from jax.experimental import pallas as pl
from jax.experimental.pallas import tpu as pltpu
from jax.sharding import PartitionSpec as P

AXES = ("grp", "sub")
LANES = 128
RADIX = 128
EMPTY = 255.0
VMEM = 16 * 1024 * 1024


def ceil_to(value, unit):
    return -(-value // unit) * unit


def nt_dot(left, right):
    return lax.dot_general(
        left, right, (((1,), (1,)), ((), ())), preferred_element_type=jnp.float32
    )


def steps(pieces):
    return sorted(range(pieces), key=lambda s: (min(s, pieces - s), s))


def in_place(array):
    return pltpu.with_memory_space_constraint(array, pltpu.VMEM)


def after(blocks, earlier):
    if not earlier:
        return blocks
    held = [in_place(x) for x in blocks]
    return list(pl.pallas_call(
        lambda *refs: None,
        out_shape=[pltpu.VMEM(x.shape, x.dtype) for x in blocks],
        in_specs=[pl.BlockSpec(memory_space=pltpu.VMEM)] * len(blocks)
        + [pl.BlockSpec(memory_space=pl.ANY)] * len(earlier),
        out_specs=[pl.BlockSpec(memory_space=pltpu.VMEM)] * len(blocks),
        input_output_aliases={i: i for i in range(len(blocks))},
        compiler_params=pltpu.CompilerParams(vmem_limit_bytes=VMEM),
        name="after",
    )(*held, *earlier))


def sizes(pieces, cap):
    return [cap] * pieces


def starts_of(counts):
    return [sum(counts[:i]) for i in range(len(counts))]


def flat(ref):
    return jnp.concatenate([ref[b : b + 1, :] for b in range(ref.shape[0])], axis=1)


def fill(first, caps, flagged, outs, unit, sorting, pick):
    rows, width = unit.shape
    target = sorting[0:1, :].astype(jnp.int32)
    digits = jnp.concatenate([sorting[...], jnp.zeros((8, rows), jnp.float32)], axis=0)
    digits = digits.astype(jnp.bfloat16)
    notes = []
    starts = starts_of(caps)
    for i, cap in enumerate(caps):
        lanes_per = ceil_to(cap, LANES)
        slots = lax.broadcasted_iota(jnp.int32, (lanes_per, rows), 0) + (first + i) * 1024
        found = jnp.where(slots == target, 1.0, 0.0).astype(jnp.bfloat16)
        pick[starts[i] : starts[i] + cap, :] = found[:cap]
        ranks = nt_dot(digits, found)
        parts = [jnp.where(ranks[3:4, :] > 0.5, ranks[1:2, :], EMPTY), ranks[2:3, :]]
        if flagged:
            parts.append(jnp.broadcast_to(sorting[4:5, :LANES], (1, LANES)))
        used = 2 * lanes_per + (LANES if flagged else 0)
        if used < width:
            parts.append(jnp.zeros((1, width - used), jnp.float32))
        notes.append(jnp.concatenate(parts, axis=1))
    last = lax.broadcasted_iota(jnp.int32, (16, 1), 0) == 15
    for at in range(0, width, 256):
        lanes = slice(at, at + 256)
        moved = jnp.dot(pick[...], unit[:, lanes], preferred_element_type=jnp.float32)
        for i, (cap, out) in enumerate(zip(caps, outs)):
            part = moved[starts[i] : starts[i] + cap]
            out[: cap - 16, lanes] = part[: cap - 16].astype(jnp.bfloat16)
            end = jnp.where(last, notes[i][:, lanes], part[cap - 16 :])
            out[cap - 16 :, lanes] = end.astype(jnp.bfloat16)


def sort_kernel(pieces, low, caps, flagged, emb, cid, rank, *refs):
    out, unit, sorting, place, held, pick, slot_ref, sem = refs
    rows, width = unit.shape
    parts = 4
    share = rows // parts
    copies = []
    for i in range(parts):
        at = pl.ds(i * share, share)
        copy = pltpu.make_async_copy(emb.at[at, :], held.at[at, :], sem.at[i])
        copy.start()
        copies.append(copy)

    plane = lax.axis_index("sub") // low
    step = flat(cid) - plane
    step = jnp.where(step < 0, step + pieces, step)
    piece = jnp.zeros(step.shape, jnp.int32)
    for p, s in enumerate(steps(pieces)):
        piece = jnp.where(step == s, p, piece)
    which = lax.broadcasted_iota(jnp.int32, (16, LANES), 0)
    upper = (
        lax.broadcasted_iota(jnp.int32, (LANES, LANES), 0)
        < lax.broadcasted_iota(jnp.int32, (LANES, LANES), 1)
    ).astype(jnp.bfloat16)
    before = jnp.zeros((16, 1), jnp.float32)
    for b in range(rows // LANES):
        lanes = slice(b * LANES, (b + 1) * LANES)
        member = piece[:, lanes] == which
        ones = member.astype(jnp.float32)
        prefix = jnp.dot(ones.astype(jnp.bfloat16), upper, preferred_element_type=jnp.float32)
        slot = jnp.sum(jnp.where(member, prefix + before, 0.0), axis=0, keepdims=True)
        slot_ref[:, lanes] = slot.astype(jnp.int32)
        before = before + jnp.sum(ones, axis=1, keepdims=True)
    slot = slot_ref[...]
    lane_starts = starts_of([ceil_to(c, LANES) for c in caps])
    spot = slot
    for p in range(1, len(caps)):
        spot = spot + jnp.where(piece == p, lane_starts[p], 0)
    place[...] = jnp.zeros(place.shape, jnp.int32)
    for b in range(rows // LANES):
        place[b : b + 1, :] = spot[:, b * LANES : (b + 1) * LANES]
    full = (jnp.max(before, axis=0, keepdims=True) > caps[0] - 1).astype(jnp.float32)
    r = flat(rank)
    sorting[0:1, :] = (piece * 1024 + slot).astype(jnp.float32)
    sorting[1:2, :] = (r // RADIX).astype(jnp.float32)
    sorting[2:3, :] = (r % RADIX).astype(jnp.float32)
    sorting[3:4, :] = jnp.ones((1, rows), jnp.float32)
    sorting[4:5, :] = jnp.broadcast_to(full, (1, rows))
    sorting[5:8, :] = jnp.zeros((3, rows), jnp.float32)

    for i in range(parts):
        copies[i].wait()

        @pl.loop(i * share // 64, (i + 1) * share // 64)
        def _(j):
            at = pl.ds(pl.multiple_of(j * 64, 64), 64)
            wide = held[at, :].astype(jnp.float32)
            scale = lax.rsqrt(jnp.sum(wide * wide, axis=1, keepdims=True) + 1e-06)
            unit[at, :] = (wide * scale).astype(jnp.bfloat16)

    fill(1, caps[1:2], flagged, [out], unit, sorting, pick)


def fill_kernel(first, caps, flagged, unit, sorting, *refs):
    fill(first, caps, flagged, refs[:-1], unit, sorting, refs[-1])


def dispatch(pieces, low, caps, flagged, emb, cid, rank):
    rows, width = emb.shape
    bf16 = jnp.bfloat16
    in_vmem = pl.BlockSpec(memory_space=pltpu.VMEM)
    one, unit, sorting, place = pl.pallas_call(
        functools.partial(sort_kernel, pieces, low, caps, flagged),
        out_shape=[
            pltpu.VMEM((caps[1], width), bf16),
            pltpu.VMEM((rows, width), bf16),
            pltpu.VMEM((8, rows), jnp.float32),
            pltpu.VMEM((8, LANES), jnp.int32),
        ],
        in_specs=[pl.BlockSpec(memory_space=pl.ANY), in_vmem, in_vmem],
        out_specs=[in_vmem] * 4,
        scratch_shapes=[
            pltpu.VMEM((rows, width), bf16),
            pltpu.VMEM((caps[1], rows), bf16),
            pltpu.VMEM((1, rows), jnp.int32),
            pltpu.SemaphoreType.DMA((4,)),
        ],
        compiler_params=pltpu.CompilerParams(vmem_limit_bytes=VMEM),
        name="sort",
    )(emb, cid.reshape(rows // LANES, LANES), rank.reshape(rows // LANES, LANES))

    def more(first, stop):
        return list(
            pl.pallas_call(
                functools.partial(fill_kernel, first, caps[first:stop], flagged),
                out_shape=[pltpu.VMEM((cap, width), bf16) for cap in caps[first:stop]],
                in_specs=[in_vmem, in_vmem],
                out_specs=[in_vmem] * (stop - first),
                scratch_shapes=[pltpu.VMEM((sum(caps[first:stop]), rows), bf16)],
                compiler_params=pltpu.CompilerParams(vmem_limit_bytes=VMEM),
                name="fill" + str(first),
            )(in_place(unit), in_place(sorting))
        )

    return more(0, 1) + [one] + more(2, len(caps)), place


def stage_kernel(p, part, caps, groups, flagged, *refs):
    new = {"all": range(groups), "home": range(2), "away": range(2, groups)}[part]
    blocks, refs = refs[: len(new)], refs[len(new) :]
    if p or part == "away":
        refs = refs[3:]
    store, limits, best, token, refs = *refs[:4], refs[4:]
    *ends, keys, cols, sem = refs
    token[...] = jnp.zeros(token.shape, jnp.float32)
    cap = caps[p]
    mine, near = 1, groups - 1
    lanes = [ceil_to(c, LANES) for c in caps]
    base = groups * starts_of(caps)[p]
    lane_base = [groups * s for s in starts_of(lanes)]
    wide = lanes[p]

    copies = []
    for g, block in zip(new, blocks):
        copy = pltpu.make_async_copy(block, store.at[pl.ds(base + g * cap, cap), :], sem.at[g])
        copy.start()
        copies.append(copy)

    lane = lax.broadcasted_iota(jnp.int32, (1, wide), 1)
    square = lax.broadcasted_iota(jnp.int32, (cap, wide), 0) == lax.broadcasted_iota(
        jnp.int32, (cap, wide), 1
    )
    flag = jnp.zeros((1, LANES), jnp.float32)
    if p == 0:
        best[...] = jnp.full(best.shape, -1.0, jnp.float32)
    cols[...] = jnp.full(cols.shape, -1.0, jnp.float32)
    for g, block in zip(new, blocks):
        note = block[cap - 16 :, :].astype(jnp.float32)[15:16, :]
        ranks = note[:, :wide] * RADIX + note[:, wide : 2 * wide]
        ranks = jnp.where(lane < cap - 1, ranks, EMPTY * RADIX)
        if flagged:
            flag = jnp.maximum(flag, note[:, 2 * wide : 2 * wide + LANES])
        at = lane_base[p] + g * wide
        limits[:, at : at + wide] = jnp.broadcast_to(ranks, (8, wide))
        column = jnp.sum(jnp.where(square, ranks, 0.0), axis=1, keepdims=True)
        keys[g * cap : (g + 1) * cap, :] = jnp.broadcast_to(column, (cap, LANES))
    if flagged:
        at = best.shape[1] - LANES
        best[:, at:] = jnp.maximum(best[:, at:], jnp.broadcast_to(flag, (8, LANES)))
    for copy in copies:
        copy.wait()

    def product(first, at, count, g, runs):
        if not runs:
            return
        query = store[pl.ds(first, count), :]
        limit = limits[0:1, pl.ds(at, count)]
        top = best[:, pl.ds(at, count)]
        for start, size, low, high in runs:
            start, size, low, high = start * cap, size * cap, low * cap, high * cap
            sims = nt_dot(store[base + start : base + start + size, :], query)
            kr = jnp.concatenate([keys[start : start + size, :]] * (count // LANES), axis=1)
            earlier = kr < limit
            if g:
                ahead = jnp.where(earlier, sims, -1.0)
                top = jnp.maximum(top, jnp.max(ahead.reshape(size // 8, 8, count), axis=0))
            if low < high:
                behind = jnp.where(earlier, -1.0, sims)[low - start : high - start]
                fold = cols[low:high, :]
                for k in range(0, count, LANES):
                    fold = jnp.maximum(fold, behind[:, k : k + LANES])
                cols[low:high, :] = fold
        if g:
            best[:, pl.ds(at, count)] = top

    def partners(g, alone):
        just_mine = [] if alone else [(mine, 1, mine, 2)]
        if part == "home":
            if g == mine:
                return [(0, 2, 1, 1 if alone else 2)]
            return just_mine
        if part == "away":
            if g == mine:
                return [(2, groups - 2, 2, groups)]
            if g == near:
                return [(2, near - 2, 2, near)]
            return [] if alone or g == 0 else [(near, 1, near, groups)]
        if g == mine:
            return [(0, near, 2, near)] if alone else [(0, groups, 1, groups)]
        if g == near:
            return [(mine, near - 1, mine, near)]
        if alone or g == 0:
            return just_mine
        return [(mine, 1, mine, 2), (near, 1, near, groups)]

    if p:

        @pl.loop(0, p)
        def _(i):
            for g in range(groups):
                at = (i * groups + g) * wide
                first = (i * groups + g) * cap
                product(
                    pl.multiple_of(first, 16), pl.multiple_of(at, LANES), wide, g, partners(g, False)
                )

    for g in range(groups):
        product(base + g * cap, lane_base[p] + g * wide, wide, g, partners(g, True))

    for g in new:
        if g:
            at = lane_base[p] + g * wide
            column = jnp.max(cols[g * cap : (g + 1) * cap, :], axis=1, keepdims=True)
            turned = jnp.max(jnp.where(square, column, -1.0), axis=0, keepdims=True)
            best[:, at : at + wide] = jnp.maximum(best[:, at : at + wide], turned)

    for g, out in enumerate(ends, start=1):
        for q, start in enumerate(starts_of(lanes)):
            at = lane_base[q] + g * lanes[q]
            row = jnp.max(best[:, at : at + lanes[q]], axis=0, keepdims=True)
            out[:, start : start + lanes[q]] = row
        out[:, sum(lanes) :] = best[0:1, best.shape[1] - LANES :]


def stage(p, part, caps, groups, flagged, blocks, carried):
    width = blocks[0].shape[1]
    lanes = sum(ceil_to(c, LANES) for c in caps)
    f32 = jnp.float32
    in_vmem = pl.BlockSpec(memory_space=pltpu.VMEM)
    kept = [
        pltpu.VMEM((groups * sum(caps) + LANES, width), jnp.bfloat16),
        pltpu.VMEM((8, groups * lanes), f32),
        pltpu.VMEM((8, groups * lanes + LANES), f32),
        jax.ShapeDtypeStruct((8, LANES), f32),
    ]
    ends = [jax.ShapeDtypeStruct((1, lanes + LANES), f32)] * (groups - 1)
    if p < len(caps) - 1 or part == "home":
        ends = []
    got = pl.pallas_call(
        functools.partial(stage_kernel, p, part, caps, groups, flagged),
        out_shape=kept + ends,
        in_specs=[in_vmem] * (len(blocks) + len(carried)),
        out_specs=[in_vmem] * (4 + len(ends)),
        scratch_shapes=[
            pltpu.VMEM((groups * caps[p], LANES), f32),
            pltpu.VMEM((groups * caps[p], LANES), f32),
            pltpu.SemaphoreType.DMA((groups,)),
        ],
        input_output_aliases={len(blocks) + i: i for i in range(len(carried))},
        cost_estimate=pl.CostEstimate(flops=0, bytes_accessed=0, transcendentals=0),
        compiler_params=pltpu.CompilerParams(vmem_limit_bytes=VMEM),
        name="stage" + str(p) + part,
    )(*[in_place(x) for x in blocks], *[in_place(x) for x in carried])
    return got[:3], got[3], got[4:]


def collect_kernel(lanes, shifts, low, place, *refs):
    rows, out = refs[:-1], refs[-1]
    plane = lax.axis_index("sub") // low
    count = len(rows)
    where = place[...]
    result = jnp.zeros((8, LANES), jnp.float32)
    for q, start in enumerate(starts_of(lanes)):
        apart = plane ^ ((plane + shifts[q]) % count)
        for first in range(start, start + lanes[q], LANES):
            back = rows[0][:, first : first + LANES]
            for s in range(1, count):
                back = jnp.where(apart == s, rows[s][:, first : first + LANES], back)
            back = jnp.broadcast_to(back, (8, LANES))
            inside = where - first
            hit = (inside >= 0) & (inside < LANES)
            taken = jnp.take_along_axis(back, jnp.where(hit, inside, 0), axis=1)
            result = jnp.where(hit, taken, result)
    out[...] = result


def collect(caps, shifts, low, place, rows):
    lanes = [ceil_to(c, LANES) for c in caps]
    return pl.pallas_call(
        functools.partial(collect_kernel, lanes, shifts, low),
        out_shape=jax.ShapeDtypeStruct((8, LANES), jnp.float32),
        in_specs=[pl.BlockSpec(memory_space=pltpu.VMEM)] * (1 + len(rows)),
        name="collect",
    )(*[in_place(x) for x in [place] + rows])


def solution(mesh):
    ngrp, nsub = mesh.shape["grp"], mesh.shape["sub"]
    low = nsub // ngrp
    pieces = ngrp
    chips = ngrp // 2

    def send(block, target):
        route = []
        for g in range(ngrp):
            for s in range(nsub):
                chip, core, plane, small = target(g // 2, g % 2, s // low, s % low)
                route.append((g * nsub + s, (chip * 2 + core) * nsub + plane * low + small))
        return lax.ppermute(block, AXES, route)

    def to_plane(block, s):
        return send(block, lambda x, c, z, y: (x, c, (z + s) % pieces, y))

    def across(block, s):
        return send(block, lambda x, c, z, y: (x, c, z ^ s, y))

    def to_twin(block):
        return send(block, lambda x, c, z, y: (x, 1 - c, z, y))

    def bit(x, j):
        return (x // (j & -j)) % 2

    def to_near(block):
        return send(block, lambda x, c, z, y: (x, c ^ (1 - y), z, 1 - y))

    def from_near(block):
        return send(block, lambda x, c, z, y: (x, c ^ y, z, 1 - y))

    def to_cross(block, j):
        return send(block, lambda x, c, z, y: (x ^ j, c ^ y ^ bit(x ^ j, j), z, y))

    def from_cross(block, j):
        return send(block, lambda x, c, z, y: (x ^ j, c ^ y ^ bit(x, j), z, y))

    def attempt(cap, flagged, embeddings, cluster_id, cluster_rank):
        rows = embeddings.shape[0]
        caps = sizes(pieces, cap)
        count = len(caps)
        step = steps(pieces)
        own, place = dispatch(pieces, low, caps, flagged, embeddings, cluster_id, cluster_rank)
        moved = [own[0]] + [None] * (count - 1)

        def leave(q, earlier):
            moved[q] = to_plane(after([own[q]], earlier)[0], step[q])

        leave(1, [])
        links, carried, tokens = [], [], []
        for p in range(count):
            earlier = links[p - 1] if p else []
            if p > 1:
                earlier = earlier + [tokens[p - 1 - 1]]
            (mine,) = after([moved[p]], earlier)
            twin = to_twin(mine)
            if p == 0:
                (mine,) = after([mine], [twin])
            cross = [to_cross(mine, j) for j in range(1, chips)]
            near = to_near(mine)
            links.append(cross + [near, twin])
            if p == 0:
                for q in range(2, pieces):
                    leave(q, [twin] if q == 2 else [])
            groups = 3 + len(cross)
            home, away = [twin, mine], cross + [near]
            if p < count - 1:
                carried, token, ends = stage(p, "all", caps, groups, flagged, home + away, carried)
            else:
                carried, token, ends = stage(p, "home", caps, groups, flagged, home, carried)
                carried, token, ends = stage(p, "away", caps, groups, flagged, away, carried)
            tokens.append(token)
        a = jnp.maximum(ends[0], from_near(ends[-1]))
        for j in range(1, chips):
            a = jnp.maximum(a, from_cross(ends[j], j))
        back = [a] + [across(a, s) for s in range(1, pieces)]
        result = collect(caps, step, low, place, back)
        return result[: rows // LANES].reshape(rows), a[0, -1]

    def body(embeddings, cluster_id, cluster_rank):
        share = embeddings.shape[0] // ngrp
        usual = ceil_to(share + 1, 16)
        most = ceil_to(2 * share + 1, 16)
        result, over = attempt(usual, True, embeddings, cluster_id, cluster_rank)

        def again():
            return attempt(most, False, embeddings, cluster_id, cluster_rank)[0]

        return lax.cond(over > 0.5, again, lambda: result)

    placed = (P(AXES, None), P(AXES), P(AXES))
    return jax.shard_map(body, mesh=mesh, in_specs=placed, out_specs=P(AXES), check_vma=False)
```

```python
import functools

import jax
import jax.numpy as jnp
from jax import lax
from jax.experimental import pallas as pl
from jax.experimental.pallas import tpu as pltpu
from jax.sharding import PartitionSpec as P

AXES = ("grp", "sub")
LANES = 128
RADIX = 128
EMPTY = 255.0
VMEM = 16 * 1024 * 1024


def ceil_to(value, unit):
    return -(-value // unit) * unit


def nt_dot(left, right):
    return lax.dot_general(
        left, right, (((1,), (1,)), ((), ())), preferred_element_type=jnp.float32
    )


def steps(pieces):
    return sorted(range(pieces), key=lambda s: (min(s, pieces - s), s))


def in_place(array):
    return pltpu.with_memory_space_constraint(array, pltpu.VMEM)


def after(blocks, earlier):
    if not earlier:
        return blocks
    held = [in_place(x) for x in blocks]
    return list(pl.pallas_call(
        lambda *refs: None,
        out_shape=[pltpu.VMEM(x.shape, x.dtype) for x in blocks],
        in_specs=[pl.BlockSpec(memory_space=pltpu.VMEM)] * len(blocks)
        + [pl.BlockSpec(memory_space=pl.ANY)] * len(earlier),
        out_specs=[pl.BlockSpec(memory_space=pltpu.VMEM)] * len(blocks),
        input_output_aliases={i: i for i in range(len(blocks))},
        compiler_params=pltpu.CompilerParams(vmem_limit_bytes=VMEM),
        name="after",
    )(*held, *earlier))


def sizes(pieces, cap):
    return [cap] * pieces


def starts_of(counts):
    return [sum(counts[:i]) for i in range(len(counts))]


def flat(ref):
    return jnp.concatenate([ref[b : b + 1, :] for b in range(ref.shape[0])], axis=1)


def fill(first, caps, flagged, outs, emb, sorting, pick, raw):
    rows, width = emb.shape
    target = sorting[0:1, :].astype(jnp.int32)
    digits = jnp.concatenate([sorting[...], jnp.zeros((8, rows), jnp.float32)], axis=0)
    digits = digits.astype(jnp.bfloat16)
    notes = []
    starts = starts_of(caps)
    for i, cap in enumerate(caps):
        lanes_per = ceil_to(cap, LANES)
        slots = lax.broadcasted_iota(jnp.int32, (lanes_per, rows), 0) + (first + i) * 1024
        found = jnp.where(slots == target, 1.0, 0.0).astype(jnp.bfloat16)
        pick[starts[i] : starts[i] + cap, :] = found[:cap]
        ranks = nt_dot(digits, found)
        parts = [jnp.where(ranks[3:4, :] > 0.5, ranks[1:2, :], EMPTY), ranks[2:3, :]]
        if flagged:
            parts.append(jnp.broadcast_to(sorting[4:5, :LANES], (1, LANES)))
        used = 2 * lanes_per + (LANES if flagged else 0)
        if used < width:
            parts.append(jnp.zeros((1, width - used), jnp.float32))
        notes.append(jnp.concatenate(parts, axis=1))
    for at in range(0, width, 256):
        lanes = slice(at, at + 256)
        raw[:, lanes] = jnp.dot(pick[...], emb[:, lanes], preferred_element_type=jnp.float32)
    last = lax.broadcasted_iota(jnp.int32, (16, 1), 0) == 15
    for i, (cap, out) in enumerate(zip(caps, outs)):
        wide = raw[starts[i] : starts[i] + cap, :]
        scale = lax.rsqrt(jnp.sum(wide * wide, axis=1, keepdims=True) + 1e-06)
        unit = wide * scale
        out[: cap - 16, :] = unit[: cap - 16].astype(jnp.bfloat16)
        out[cap - 16 :, :] = jnp.where(last, notes[i], unit[cap - 16 :]).astype(jnp.bfloat16)


def sort_kernel(pieces, low, caps, flagged, emb, cid, rank, *refs):
    out, held, sorting, place, pick, raw, slot_ref, sem = refs
    rows, width = held.shape
    parts = 4
    share = rows // parts
    copies = []
    for i in range(parts):
        at = pl.ds(i * share, share)
        copy = pltpu.make_async_copy(emb.at[at, :], held.at[at, :], sem.at[i])
        copy.start()
        copies.append(copy)

    plane = lax.axis_index("sub") // low
    step = flat(cid) - plane
    step = jnp.where(step < 0, step + pieces, step)
    piece = jnp.zeros(step.shape, jnp.int32)
    for p, s in enumerate(steps(pieces)):
        piece = jnp.where(step == s, p, piece)
    which = lax.broadcasted_iota(jnp.int32, (16, LANES), 0)
    upper = (
        lax.broadcasted_iota(jnp.int32, (LANES, LANES), 0)
        < lax.broadcasted_iota(jnp.int32, (LANES, LANES), 1)
    ).astype(jnp.bfloat16)
    before = jnp.zeros((16, 1), jnp.float32)
    for b in range(rows // LANES):
        lanes = slice(b * LANES, (b + 1) * LANES)
        member = piece[:, lanes] == which
        ones = member.astype(jnp.float32)
        prefix = jnp.dot(ones.astype(jnp.bfloat16), upper, preferred_element_type=jnp.float32)
        slot = jnp.sum(jnp.where(member, prefix + before, 0.0), axis=0, keepdims=True)
        slot_ref[:, lanes] = slot.astype(jnp.int32)
        before = before + jnp.sum(ones, axis=1, keepdims=True)
    slot = slot_ref[...]
    lane_starts = starts_of([ceil_to(c, LANES) for c in caps])
    spot = slot
    for p in range(1, len(caps)):
        spot = spot + jnp.where(piece == p, lane_starts[p], 0)
    place[...] = jnp.zeros(place.shape, jnp.int32)
    for b in range(rows // LANES):
        place[b : b + 1, :] = spot[:, b * LANES : (b + 1) * LANES]
    full = (jnp.max(before, axis=0, keepdims=True) > caps[0] - 1).astype(jnp.float32)
    r = flat(rank)
    sorting[0:1, :] = (piece * 1024 + slot).astype(jnp.float32)
    sorting[1:2, :] = (r // RADIX).astype(jnp.float32)
    sorting[2:3, :] = (r % RADIX).astype(jnp.float32)
    sorting[3:4, :] = jnp.ones((1, rows), jnp.float32)
    sorting[4:5, :] = jnp.broadcast_to(full, (1, rows))
    sorting[5:8, :] = jnp.zeros((3, rows), jnp.float32)

    for copy in copies:
        copy.wait()
    fill(1, caps[1:2], flagged, [out], held, sorting, pick, raw)


def fill_kernel(first, caps, flagged, emb, sorting, *refs):
    fill(first, caps, flagged, refs[:-2], emb, sorting, refs[-2], refs[-1])


def dispatch(pieces, low, caps, flagged, emb, cid, rank):
    rows, width = emb.shape
    bf16 = jnp.bfloat16
    in_vmem = pl.BlockSpec(memory_space=pltpu.VMEM)
    one, held, sorting, place = pl.pallas_call(
        functools.partial(sort_kernel, pieces, low, caps, flagged),
        out_shape=[
            pltpu.VMEM((caps[1], width), bf16),
            pltpu.VMEM((rows, width), bf16),
            pltpu.VMEM((8, rows), jnp.float32),
            pltpu.VMEM((8, LANES), jnp.int32),
        ],
        in_specs=[pl.BlockSpec(memory_space=pl.ANY), in_vmem, in_vmem],
        out_specs=[in_vmem] * 4,
        scratch_shapes=[
            pltpu.VMEM((caps[1], rows), bf16),
            pltpu.VMEM((caps[1], width), jnp.float32),
            pltpu.VMEM((1, rows), jnp.int32),
            pltpu.SemaphoreType.DMA((4,)),
        ],
        compiler_params=pltpu.CompilerParams(vmem_limit_bytes=VMEM),
        name="sort",
    )(emb, cid.reshape(rows // LANES, LANES), rank.reshape(rows // LANES, LANES))

    def more(first, stop):
        return list(
            pl.pallas_call(
                functools.partial(fill_kernel, first, caps[first:stop], flagged),
                out_shape=[pltpu.VMEM((cap, width), bf16) for cap in caps[first:stop]],
                in_specs=[in_vmem, in_vmem],
                out_specs=[in_vmem] * (stop - first),
                scratch_shapes=[
                    pltpu.VMEM((sum(caps[first:stop]), rows), bf16),
                    pltpu.VMEM((sum(caps[first:stop]), width), jnp.float32),
                ],
                compiler_params=pltpu.CompilerParams(vmem_limit_bytes=VMEM),
                name="fill" + str(first),
            )(in_place(held), in_place(sorting))
        )

    return more(0, 1) + [one] + more(2, len(caps)), place


def stage_kernel(p, part, caps, groups, flagged, *refs):
    new = {"all": range(groups), "home": range(2), "away": range(2, groups)}[part]
    blocks, refs = refs[: len(new)], refs[len(new) :]
    if p or part == "away":
        refs = refs[3:]
    store, limits, best, token, refs = *refs[:4], refs[4:]
    *ends, keys, cols, sem = refs
    token[...] = jnp.zeros(token.shape, jnp.float32)
    cap = caps[p]
    mine, near = 1, groups - 1
    lanes = [ceil_to(c, LANES) for c in caps]
    base = groups * starts_of(caps)[p]
    lane_base = [groups * s for s in starts_of(lanes)]
    wide = lanes[p]

    copies = []
    for g, block in zip(new, blocks):
        copy = pltpu.make_async_copy(block, store.at[pl.ds(base + g * cap, cap), :], sem.at[g])
        copy.start()
        copies.append(copy)

    lane = lax.broadcasted_iota(jnp.int32, (1, wide), 1)
    square = lax.broadcasted_iota(jnp.int32, (cap, wide), 0) == lax.broadcasted_iota(
        jnp.int32, (cap, wide), 1
    )
    flag = jnp.zeros((1, LANES), jnp.float32)
    if p == 0 and part != "away":
        best[...] = jnp.full(best.shape, -1.0, jnp.float32)
    cols[...] = jnp.full(cols.shape, -1.0, jnp.float32)
    for g, block in zip(new, blocks):
        note = block[cap - 16 :, :].astype(jnp.float32)[15:16, :]
        ranks = note[:, :wide] * RADIX + note[:, wide : 2 * wide]
        ranks = jnp.where(lane < cap - 1, ranks, EMPTY * RADIX)
        if flagged:
            flag = jnp.maximum(flag, note[:, 2 * wide : 2 * wide + LANES])
        at = lane_base[p] + g * wide
        limits[:, at : at + wide] = jnp.broadcast_to(ranks, (8, wide))
        column = jnp.sum(jnp.where(square, ranks, 0.0), axis=1, keepdims=True)
        keys[g * cap : (g + 1) * cap, :] = jnp.broadcast_to(column, (cap, LANES))
    if flagged:
        at = best.shape[1] - LANES
        best[:, at:] = jnp.maximum(best[:, at:], jnp.broadcast_to(flag, (8, LANES)))
    for copy in copies:
        copy.wait()

    def product(first, at, count, g, runs):
        if not runs:
            return
        query = store[pl.ds(first, count), :]
        limit = limits[0:1, pl.ds(at, count)]
        top = best[:, pl.ds(at, count)]
        for start, size, low, high in runs:
            start, size, low, high = start * cap, size * cap, low * cap, high * cap
            sims = nt_dot(store[base + start : base + start + size, :], query)
            kr = jnp.concatenate([keys[start : start + size, :]] * (count // LANES), axis=1)
            earlier = kr < limit
            if g:
                ahead = jnp.where(earlier, sims, -1.0)
                top = jnp.maximum(top, jnp.max(ahead.reshape(size // 8, 8, count), axis=0))
            if low < high:
                behind = jnp.where(earlier, -1.0, sims)[low - start : high - start]
                fold = cols[low:high, :]
                for k in range(0, count, LANES):
                    fold = jnp.maximum(fold, behind[:, k : k + LANES])
                cols[low:high, :] = fold
        if g:
            best[:, pl.ds(at, count)] = top

    def partners(g, alone):
        just_mine = [] if alone else [(mine, 1, mine, 2)]
        if part == "home":
            if g == mine:
                return [(0, 2, 1, 1 if alone else 2)]
            return just_mine
        if part == "away":
            if g == mine:
                return [(2, groups - 2, 2, groups)]
            if g == near:
                return [(2, near - 2, 2, near)]
            return [] if alone or g == 0 else [(near, 1, near, groups)]
        if g == mine:
            return [(0, near, 2, near)] if alone else [(0, groups, 1, groups)]
        if g == near:
            return [(mine, near - 1, mine, near)]
        if alone or g == 0:
            return just_mine
        return [(mine, 1, mine, 2), (near, 1, near, groups)]

    def old(i):
        for g in range(groups):
            at = (i * groups + g) * wide
            first = (i * groups + g) * cap
            if part != "away":
                first, at = pl.multiple_of(first, 16), pl.multiple_of(at, LANES)
            product(first, at, wide, g, partners(g, False))

    if part == "away":
        for i in range(p):
            old(i)
    elif p:
        pl.loop(0, p)(old)

    for g in range(groups):
        product(base + g * cap, lane_base[p] + g * wide, wide, g, partners(g, True))

    for g in new:
        if g:
            at = lane_base[p] + g * wide
            column = jnp.max(cols[g * cap : (g + 1) * cap, :], axis=1, keepdims=True)
            turned = jnp.max(jnp.where(square, column, -1.0), axis=0, keepdims=True)
            best[:, at : at + wide] = jnp.maximum(best[:, at : at + wide], turned)

    for g, out in enumerate(ends, start=1):
        for q, start in enumerate(starts_of(lanes)):
            at = lane_base[q] + g * lanes[q]
            row = jnp.max(best[:, at : at + lanes[q]], axis=0, keepdims=True)
            out[:, start : start + lanes[q]] = row
        out[:, sum(lanes) :] = best[0:1, best.shape[1] - LANES :]


def stage(p, part, caps, groups, flagged, blocks, carried):
    width = blocks[0].shape[1]
    lanes = sum(ceil_to(c, LANES) for c in caps)
    f32 = jnp.float32
    in_vmem = pl.BlockSpec(memory_space=pltpu.VMEM)
    kept = [
        pltpu.VMEM((groups * sum(caps) + LANES, width), jnp.bfloat16),
        pltpu.VMEM((8, groups * lanes), f32),
        pltpu.VMEM((8, groups * lanes + LANES), f32),
        jax.ShapeDtypeStruct((8, LANES), f32),
    ]
    ends = [jax.ShapeDtypeStruct((1, lanes + LANES), f32)] * (groups - 1)
    if p < len(caps) - 1 or part == "home":
        ends = []
    got = pl.pallas_call(
        functools.partial(stage_kernel, p, part, caps, groups, flagged),
        out_shape=kept + ends,
        in_specs=[in_vmem] * (len(blocks) + len(carried)),
        out_specs=[in_vmem] * (4 + len(ends)),
        scratch_shapes=[
            pltpu.VMEM((groups * caps[p], LANES), f32),
            pltpu.VMEM((groups * caps[p], LANES), f32),
            pltpu.SemaphoreType.DMA((groups,)),
        ],
        input_output_aliases={len(blocks) + i: i for i in range(len(carried))},
        cost_estimate=pl.CostEstimate(flops=0, bytes_accessed=0, transcendentals=0),
        compiler_params=pltpu.CompilerParams(vmem_limit_bytes=VMEM),
        name="stage" + str(p) + part,
    )(*[in_place(x) for x in blocks], *[in_place(x) for x in carried])
    return got[:3], got[3], got[4:]


def collect_kernel(lanes, shifts, low, place, *refs):
    rows, out = refs[:-1], refs[-1]
    plane = lax.axis_index("sub") // low
    count = len(rows)
    where = place[...]
    result = jnp.zeros((8, LANES), jnp.float32)
    for q, start in enumerate(starts_of(lanes)):
        apart = plane ^ ((plane + shifts[q]) % count)
        for first in range(start, start + lanes[q], LANES):
            back = rows[0][:, first : first + LANES]
            for s in range(1, count):
                back = jnp.where(apart == s, rows[s][:, first : first + LANES], back)
            back = jnp.broadcast_to(back, (8, LANES))
            inside = where - first
            hit = (inside >= 0) & (inside < LANES)
            taken = jnp.take_along_axis(back, jnp.where(hit, inside, 0), axis=1)
            result = jnp.where(hit, taken, result)
    out[...] = result


def collect(caps, shifts, low, place, rows):
    lanes = [ceil_to(c, LANES) for c in caps]
    return pl.pallas_call(
        functools.partial(collect_kernel, lanes, shifts, low),
        out_shape=jax.ShapeDtypeStruct((8, LANES), jnp.float32),
        in_specs=[pl.BlockSpec(memory_space=pltpu.VMEM)] * (1 + len(rows)),
        name="collect",
    )(*[in_place(x) for x in [place] + rows])


def solution(mesh):
    ngrp, nsub = mesh.shape["grp"], mesh.shape["sub"]
    low = nsub // ngrp
    pieces = ngrp
    chips = ngrp // 2

    def send(block, target):
        route = []
        for g in range(ngrp):
            for s in range(nsub):
                chip, core, plane, small = target(g // 2, g % 2, s // low, s % low)
                route.append((g * nsub + s, (chip * 2 + core) * nsub + plane * low + small))
        return lax.ppermute(block, AXES, route)

    def to_plane(block, s):
        return send(block, lambda x, c, z, y: (x, c, (z + s) % pieces, y))

    def across(block, s):
        return send(block, lambda x, c, z, y: (x, c, z ^ s, y))

    def to_twin(block):
        return send(block, lambda x, c, z, y: (x, 1 - c, z, y))

    def bit(x, j):
        return (x // (j & -j)) % 2

    def to_near(block):
        return send(block, lambda x, c, z, y: (x, c ^ (1 - y), z, 1 - y))

    def from_near(block):
        return send(block, lambda x, c, z, y: (x, c ^ y, z, 1 - y))

    def to_cross(block, j):
        return send(block, lambda x, c, z, y: (x ^ j, c ^ y ^ bit(x ^ j, j), z, y))

    def from_cross(block, j):
        return send(block, lambda x, c, z, y: (x ^ j, c ^ y ^ bit(x, j), z, y))

    def attempt(cap, flagged, embeddings, cluster_id, cluster_rank):
        rows = embeddings.shape[0]
        caps = sizes(pieces, cap)
        count = len(caps)
        step = steps(pieces)
        own, place = dispatch(pieces, low, caps, flagged, embeddings, cluster_id, cluster_rank)
        moved = [own[0]] + [None] * (count - 1)

        def leave(q, earlier):
            moved[q] = to_plane(after([own[q]], earlier)[0], step[q])

        leave(1, [])
        links, carried, tokens = [], [], []
        for p in range(count):
            earlier = links[p - 2] if p >= 2 else []
            if p > 1:
                earlier = earlier + [tokens[p - 1 - 1]]
            (mine,) = after([moved[p]], earlier)
            twin = to_twin(mine)
            if p == 0:
                (mine,) = after([mine], [twin])
            cross = [to_cross(mine, j) for j in range(1, chips)]
            near = to_near(mine)
            links.append(cross + [near, twin])
            groups = 3 + len(cross)
            home, away = [twin, mine], cross + [near]
            if p in (count - 1,):
                carried, token, ends = stage(p, "home", caps, groups, flagged, home, carried)
                if p == 0:
                    for q in range(2, pieces):
                        leave(q, [token] if q == 2 else [])
                carried, token, ends = stage(p, "away", caps, groups, flagged, away, carried)
            else:
                if p == 0:
                    for q in range(2, pieces):
                        leave(q, [twin] if q == 2 else [])
                carried, token, ends = stage(p, "all", caps, groups, flagged, home + away, carried)
            tokens.append(token)
        a = jnp.maximum(ends[0], from_near(ends[-1]))
        for j in range(1, chips):
            a = jnp.maximum(a, from_cross(ends[j], j))
        back = [a] + [across(a, s) for s in range(1, pieces)]
        result = collect(caps, step, low, place, back)
        return result[: rows // LANES].reshape(rows), a[0, -1]

    def body(embeddings, cluster_id, cluster_rank):
        share = embeddings.shape[0] // ngrp
        usual = ceil_to(share + 1, 16)
        most = ceil_to(2 * share + 1, 16)
        result, over = attempt(usual, True, embeddings, cluster_id, cluster_rank)

        def again():
            return attempt(most, False, embeddings, cluster_id, cluster_rank)[0]

        return lax.cond(over > 0.5, again, lambda: result)

    placed = (P(AXES, None), P(AXES), P(AXES))
    return jax.shard_map(body, mesh=mesh, in_specs=placed, out_specs=P(AXES), check_vma=False)
```

```python
import functools

import jax
import jax.numpy as jnp
from jax import lax
from jax.experimental import pallas as pl
from jax.experimental.pallas import tpu as pltpu
from jax.sharding import PartitionSpec as P

AXES = ("grp", "sub")
LANES = 128
RADIX = 128
EMPTY = 255.0
VMEM = 16 * 1024 * 1024


def ceil_to(value, unit):
    return -(-value // unit) * unit


def nt_dot(left, right):
    return lax.dot_general(
        left, right, (((1,), (1,)), ((), ())), preferred_element_type=jnp.float32
    )


def steps(pieces):
    bits = (pieces - 1).bit_length()
    return [sum((p >> i & 1) << (bits - 1 - i) for i in range(bits)) for p in range(pieces)]


def in_place(array):
    return pltpu.with_memory_space_constraint(array, pltpu.VMEM)


def after(blocks, earlier):
    if not earlier:
        return blocks
    held = [in_place(x) for x in blocks]
    return list(pl.pallas_call(
        lambda *refs: None,
        out_shape=[pltpu.VMEM(x.shape, x.dtype) for x in blocks],
        in_specs=[pl.BlockSpec(memory_space=pltpu.VMEM)] * len(blocks)
        + [pl.BlockSpec(memory_space=pl.ANY)] * len(earlier),
        out_specs=[pl.BlockSpec(memory_space=pltpu.VMEM)] * len(blocks),
        input_output_aliases={i: i for i in range(len(blocks))},
        compiler_params=pltpu.CompilerParams(vmem_limit_bytes=VMEM),
        name="after",
    )(*held, *earlier))


def sizes(pieces, cap):
    return [cap] * pieces


def starts_of(counts):
    return [sum(counts[:i]) for i in range(len(counts))]


def flat(ref):
    return jnp.concatenate([ref[b : b + 1, :] for b in range(ref.shape[0])], axis=1)


def fill(first, caps, flagged, outs, emb, sorting, pick, raw):
    rows, width = emb.shape
    target = sorting[0:1, :].astype(jnp.int32)
    digits = jnp.concatenate([sorting[...], jnp.zeros((8, rows), jnp.float32)], axis=0)
    digits = digits.astype(jnp.bfloat16)
    notes = []
    starts = starts_of(caps)
    for i, cap in enumerate(caps):
        lanes_per = ceil_to(cap, LANES)
        slots = lax.broadcasted_iota(jnp.int32, (lanes_per, rows), 0) + (first + i) * 1024
        found = jnp.where(slots == target, 1.0, 0.0).astype(jnp.bfloat16)
        pick[starts[i] : starts[i] + cap, :] = found[:cap]
        ranks = nt_dot(digits, found)
        parts = [jnp.where(ranks[3:4, :] > 0.5, ranks[1:2, :], EMPTY), ranks[2:3, :]]
        if flagged:
            parts.append(jnp.broadcast_to(sorting[4:5, :LANES], (1, LANES)))
        used = 2 * lanes_per + (LANES if flagged else 0)
        if used < width:
            parts.append(jnp.zeros((1, width - used), jnp.float32))
        notes.append(jnp.concatenate(parts, axis=1))
    for at in range(0, width, 256):
        lanes = slice(at, at + 256)
        raw[:, lanes] = jnp.dot(pick[...], emb[:, lanes], preferred_element_type=jnp.float32)
    last = lax.broadcasted_iota(jnp.int32, (16, 1), 0) == 15
    for i, (cap, out) in enumerate(zip(caps, outs)):
        wide = raw[starts[i] : starts[i] + cap, :]
        scale = lax.rsqrt(jnp.sum(wide * wide, axis=1, keepdims=True) + 1e-06)
        unit = wide * scale
        out[: cap - 16, :] = unit[: cap - 16].astype(jnp.bfloat16)
        out[cap - 16 :, :] = jnp.where(last, notes[i], unit[cap - 16 :]).astype(jnp.bfloat16)


def sort_kernel(pieces, low, caps, flagged, emb, cid, rank, *refs):
    out, held, sorting, place, pick, raw, slot_ref, sem = refs
    rows, width = held.shape
    parts = 4
    share = rows // parts
    copies = []
    for i in range(parts):
        at = pl.ds(i * share, share)
        copy = pltpu.make_async_copy(emb.at[at, :], held.at[at, :], sem.at[i])
        copy.start()
        copies.append(copy)

    plane = lax.axis_index("sub") // low
    step = flat(cid) ^ plane
    piece = jnp.zeros(step.shape, jnp.int32)
    for p, s in enumerate(steps(pieces)):
        piece = jnp.where(step == s, p, piece)
    which = lax.broadcasted_iota(jnp.int32, (16, LANES), 0)
    upper = (
        lax.broadcasted_iota(jnp.int32, (LANES, LANES), 0)
        < lax.broadcasted_iota(jnp.int32, (LANES, LANES), 1)
    ).astype(jnp.bfloat16)
    before = jnp.zeros((16, 1), jnp.float32)
    for b in range(rows // LANES):
        lanes = slice(b * LANES, (b + 1) * LANES)
        member = piece[:, lanes] == which
        ones = member.astype(jnp.float32)
        prefix = jnp.dot(ones.astype(jnp.bfloat16), upper, preferred_element_type=jnp.float32)
        slot = jnp.sum(jnp.where(member, prefix + before, 0.0), axis=0, keepdims=True)
        slot_ref[:, lanes] = slot.astype(jnp.int32)
        before = before + jnp.sum(ones, axis=1, keepdims=True)
    slot = slot_ref[...]
    lane_starts = starts_of([ceil_to(c, LANES) for c in caps])
    spot = slot
    for p in range(1, len(caps)):
        spot = spot + jnp.where(piece == p, lane_starts[p], 0)
    place[...] = jnp.zeros(place.shape, jnp.int32)
    for b in range(rows // LANES):
        place[b : b + 1, :] = spot[:, b * LANES : (b + 1) * LANES]
    full = (jnp.max(before, axis=0, keepdims=True) > caps[0] - 1).astype(jnp.float32)
    r = flat(rank)
    sorting[0:1, :] = (piece * 1024 + slot).astype(jnp.float32)
    sorting[1:2, :] = (r // RADIX).astype(jnp.float32)
    sorting[2:3, :] = (r % RADIX).astype(jnp.float32)
    sorting[3:4, :] = jnp.ones((1, rows), jnp.float32)
    sorting[4:5, :] = jnp.broadcast_to(full, (1, rows))
    sorting[5:8, :] = jnp.zeros((3, rows), jnp.float32)

    for copy in copies:
        copy.wait()
    fill(1, caps[1:2], flagged, [out], held, sorting, pick, raw)


def fill_kernel(first, caps, flagged, emb, sorting, *refs):
    fill(first, caps, flagged, refs[:-2], emb, sorting, refs[-2], refs[-1])


def dispatch(pieces, low, caps, flagged, emb, cid, rank):
    rows, width = emb.shape
    bf16 = jnp.bfloat16
    in_vmem = pl.BlockSpec(memory_space=pltpu.VMEM)
    one, held, sorting, place = pl.pallas_call(
        functools.partial(sort_kernel, pieces, low, caps, flagged),
        out_shape=[
            pltpu.VMEM((caps[1], width), bf16),
            pltpu.VMEM((rows, width), bf16),
            pltpu.VMEM((8, rows), jnp.float32),
            pltpu.VMEM((8, LANES), jnp.int32),
        ],
        in_specs=[pl.BlockSpec(memory_space=pl.ANY), in_vmem, in_vmem],
        out_specs=[in_vmem] * 4,
        scratch_shapes=[
            pltpu.VMEM((caps[1], rows), bf16),
            pltpu.VMEM((caps[1], width), jnp.float32),
            pltpu.VMEM((1, rows), jnp.int32),
            pltpu.SemaphoreType.DMA((4,)),
        ],
        compiler_params=pltpu.CompilerParams(vmem_limit_bytes=VMEM),
        name="sort",
    )(emb, cid.reshape(rows // LANES, LANES), rank.reshape(rows // LANES, LANES))

    def more(first, stop):
        return list(
            pl.pallas_call(
                functools.partial(fill_kernel, first, caps[first:stop], flagged),
                out_shape=[pltpu.VMEM((cap, width), bf16) for cap in caps[first:stop]],
                in_specs=[in_vmem, in_vmem],
                out_specs=[in_vmem] * (stop - first),
                scratch_shapes=[
                    pltpu.VMEM((sum(caps[first:stop]), rows), bf16),
                    pltpu.VMEM((sum(caps[first:stop]), width), jnp.float32),
                ],
                compiler_params=pltpu.CompilerParams(vmem_limit_bytes=VMEM),
                name="fill" + str(first),
            )(in_place(held), in_place(sorting))
        )

    return more(0, 1) + [one] + more(2, len(caps)), place


def stage_kernel(p, part, caps, groups, flagged, *refs):
    new = {"all": range(groups), "home": range(2), "away": range(2, groups)}[part]
    blocks, refs = refs[: len(new)], refs[len(new) :]
    if p or part == "away":
        refs = refs[3:]
    store, limits, best, token, refs = *refs[:4], refs[4:]
    *ends, keys, cols, sem = refs
    token[...] = jnp.zeros(token.shape, jnp.float32)
    cap = caps[p]
    mine, near = 1, groups - 1
    lanes = [ceil_to(c, LANES) for c in caps]
    base = groups * starts_of(caps)[p]
    lane_base = [groups * s for s in starts_of(lanes)]
    wide = lanes[p]

    copies = []
    for g, block in zip(new, blocks):
        copy = pltpu.make_async_copy(block, store.at[pl.ds(base + g * cap, cap), :], sem.at[g])
        copy.start()
        copies.append(copy)

    lane = lax.broadcasted_iota(jnp.int32, (1, wide), 1)
    square = lax.broadcasted_iota(jnp.int32, (cap, wide), 0) == lax.broadcasted_iota(
        jnp.int32, (cap, wide), 1
    )
    flag = jnp.zeros((1, LANES), jnp.float32)
    if p == 0 and part != "away":
        best[...] = jnp.full(best.shape, -1.0, jnp.float32)
    cols[...] = jnp.full(cols.shape, -1.0, jnp.float32)
    for g, block in zip(new, blocks):
        note = block[cap - 16 :, :].astype(jnp.float32)[15:16, :]
        ranks = note[:, :wide] * RADIX + note[:, wide : 2 * wide]
        ranks = jnp.where(lane < cap - 1, ranks, EMPTY * RADIX)
        if flagged:
            flag = jnp.maximum(flag, note[:, 2 * wide : 2 * wide + LANES])
        at = lane_base[p] + g * wide
        limits[:, at : at + wide] = jnp.broadcast_to(ranks, (8, wide))
        column = jnp.sum(jnp.where(square, ranks, 0.0), axis=1, keepdims=True)
        keys[g * cap : (g + 1) * cap, :] = jnp.broadcast_to(column, (cap, LANES))
    if flagged:
        at = best.shape[1] - LANES
        best[:, at:] = jnp.maximum(best[:, at:], jnp.broadcast_to(flag, (8, LANES)))
    for copy in copies:
        copy.wait()

    def product(first, at, count, g, runs):
        if not runs:
            return
        query = store[pl.ds(first, count), :]
        limit = limits[0:1, pl.ds(at, count)]
        top = best[:, pl.ds(at, count)]
        for start, size, low, high in runs:
            start, size, low, high = start * cap, size * cap, low * cap, high * cap
            sims = nt_dot(store[base + start : base + start + size, :], query)
            kr = jnp.concatenate([keys[start : start + size, :]] * (count // LANES), axis=1)
            earlier = kr < limit
            if g:
                ahead = jnp.where(earlier, sims, -1.0)
                top = jnp.maximum(top, jnp.max(ahead.reshape(size // 8, 8, count), axis=0))
            if low < high:
                behind = jnp.where(earlier, -1.0, sims)[low - start : high - start]
                fold = cols[low:high, :]
                for k in range(0, count, LANES):
                    fold = jnp.maximum(fold, behind[:, k : k + LANES])
                cols[low:high, :] = fold
        if g:
            best[:, pl.ds(at, count)] = top

    def partners(g, alone):
        just_mine = [] if alone else [(mine, 1, mine, 2)]
        if part == "home":
            if g == mine:
                return [(0, 2, 1, 1 if alone else 2)]
            return just_mine
        if part == "away":
            if g == mine:
                return [(2, groups - 2, 2, groups)]
            if g == near:
                return [(2, near - 2, 2, near)]
            return [] if alone or g == 0 else [(near, 1, near, groups)]
        if g == mine:
            return [(0, near, 2, near)] if alone else [(0, groups, 1, groups)]
        if g == near:
            return [(mine, near - 1, mine, near)]
        if alone or g == 0:
            return just_mine
        return [(mine, 1, mine, 2), (near, 1, near, groups)]

    def old(i):
        for g in range(groups):
            at = (i * groups + g) * wide
            first = (i * groups + g) * cap
            if part != "away":
                first, at = pl.multiple_of(first, 16), pl.multiple_of(at, LANES)
            product(first, at, wide, g, partners(g, False))

    if part == "away":
        for i in range(p):
            old(i)
    elif p:
        pl.loop(0, p)(old)

    for g in range(groups):
        product(base + g * cap, lane_base[p] + g * wide, wide, g, partners(g, True))

    for g in new:
        if g:
            at = lane_base[p] + g * wide
            column = jnp.max(cols[g * cap : (g + 1) * cap, :], axis=1, keepdims=True)
            turned = jnp.max(jnp.where(square, column, -1.0), axis=0, keepdims=True)
            best[:, at : at + wide] = jnp.maximum(best[:, at : at + wide], turned)

    for g, out in enumerate(ends, start=1):
        for q, start in enumerate(starts_of(lanes)):
            at = lane_base[q] + g * lanes[q]
            row = jnp.max(best[:, at : at + lanes[q]], axis=0, keepdims=True)
            out[:, start : start + lanes[q]] = row
        out[:, sum(lanes) :] = best[0:1, best.shape[1] - LANES :]


def stage(p, part, caps, groups, flagged, blocks, carried):
    width = blocks[0].shape[1]
    lanes = sum(ceil_to(c, LANES) for c in caps)
    f32 = jnp.float32
    in_vmem = pl.BlockSpec(memory_space=pltpu.VMEM)
    kept = [
        pltpu.VMEM((groups * sum(caps) + LANES, width), jnp.bfloat16),
        pltpu.VMEM((8, groups * lanes), f32),
        pltpu.VMEM((8, groups * lanes + LANES), f32),
        jax.ShapeDtypeStruct((8, LANES), f32),
    ]
    ends = [jax.ShapeDtypeStruct((1, lanes + LANES), f32)] * (groups - 1)
    if p < len(caps) - 1 or part == "home":
        ends = []
    got = pl.pallas_call(
        functools.partial(stage_kernel, p, part, caps, groups, flagged),
        out_shape=kept + ends,
        in_specs=[in_vmem] * (len(blocks) + len(carried)),
        out_specs=[in_vmem] * (4 + len(ends)),
        scratch_shapes=[
            pltpu.VMEM((groups * caps[p], LANES), f32),
            pltpu.VMEM((groups * caps[p], LANES), f32),
            pltpu.SemaphoreType.DMA((groups,)),
        ],
        input_output_aliases={len(blocks) + i: i for i in range(len(carried))},
        cost_estimate=pl.CostEstimate(flops=0, bytes_accessed=0, transcendentals=0),
        compiler_params=pltpu.CompilerParams(vmem_limit_bytes=VMEM),
        name="stage" + str(p) + part,
    )(*[in_place(x) for x in blocks], *[in_place(x) for x in carried])
    return got[:3], got[3], got[4:]


def collect_kernel(lanes, step, place, *refs):
    rows, out = refs[:-1], refs[-1]
    where = place[...]
    result = jnp.zeros((8, LANES), jnp.float32)
    for q, start in enumerate(starts_of(lanes)):
        for first in range(start, start + lanes[q], LANES):
            back = jnp.broadcast_to(rows[step[q]][:, first : first + LANES], (8, LANES))
            inside = where - first
            hit = (inside >= 0) & (inside < LANES)
            taken = jnp.take_along_axis(back, jnp.where(hit, inside, 0), axis=1)
            result = jnp.where(hit, taken, result)
    out[...] = result


def collect(caps, step, place, rows):
    lanes = [ceil_to(c, LANES) for c in caps]
    return pl.pallas_call(
        functools.partial(collect_kernel, lanes, step),
        out_shape=jax.ShapeDtypeStruct((8, LANES), jnp.float32),
        in_specs=[pl.BlockSpec(memory_space=pltpu.VMEM)] * (1 + len(rows)),
        name="collect",
    )(*[in_place(x) for x in [place] + rows])


def solution(mesh):
    ngrp, nsub = mesh.shape["grp"], mesh.shape["sub"]
    low = nsub // ngrp
    pieces = ngrp
    chips = ngrp // 2

    def send(block, target):
        route = []
        for g in range(ngrp):
            for s in range(nsub):
                chip, core, plane, small = target(g // 2, g % 2, s // low, s % low)
                route.append((g * nsub + s, (chip * 2 + core) * nsub + plane * low + small))
        return lax.ppermute(block, AXES, route)

    def to_plane(block, s):
        return send(block, lambda x, c, z, y: (x, c, z ^ s, y))

    def to_twin(block):
        return send(block, lambda x, c, z, y: (x, 1 - c, z, y))

    def bit(x, j):
        return (x // (j & -j)) % 2

    def to_near(block):
        return send(block, lambda x, c, z, y: (x, c ^ (1 - y), z, 1 - y))

    def from_near(block):
        return send(block, lambda x, c, z, y: (x, c ^ y, z, 1 - y))

    def to_cross(block, j):
        return send(block, lambda x, c, z, y: (x ^ j, c ^ y ^ bit(x ^ j, j), z, y))

    def from_cross(block, j):
        return send(block, lambda x, c, z, y: (x ^ j, c ^ y ^ bit(x, j), z, y))

    def attempt(cap, flagged, embeddings, cluster_id, cluster_rank):
        rows = embeddings.shape[0]
        caps = sizes(pieces, cap)
        count = len(caps)
        step = steps(pieces)
        own, place = dispatch(pieces, low, caps, flagged, embeddings, cluster_id, cluster_rank)
        moved = [own[0]] + [None] * (count - 1)

        def leave(q, earlier):
            moved[q] = to_plane(after([own[q]], earlier)[0], step[q])

        leave(1, [])
        links, carried, tokens = [], [], []
        for p in range(count):
            earlier = links[p - 2] if p >= 2 else []
            if p > 1:
                earlier = earlier + [tokens[p - 1 - 1]]
            (mine,) = after([moved[p]], earlier)
            twin = to_twin(mine)
            if p == 0:
                (mine,) = after([mine], [twin])
            cross = [to_cross(mine, j) for j in range(1, chips)]
            near = to_near(mine)
            links.append(cross + [near, twin])
            groups = 3 + len(cross)
            home, away = [twin, mine], cross + [near]
            if p in (count - 1,):
                carried, token, ends = stage(p, "home", caps, groups, flagged, home, carried)
                if p == 0:
                    for q in range(2, pieces):
                        leave(q, [token] if q == 2 else [])
                carried, token, ends = stage(p, "away", caps, groups, flagged, away, carried)
            else:
                if p == 0:
                    for q in range(2, pieces):
                        leave(q, [twin] if q == 2 else [])
                carried, token, ends = stage(p, "all", caps, groups, flagged, home + away, carried)
            tokens.append(token)
        a = jnp.maximum(ends[0], from_near(ends[-1]))
        for j in range(1, chips):
            a = jnp.maximum(a, from_cross(ends[j], j))
        back = [a] + [to_plane(a, s) for s in range(1, pieces)]
        result = collect(caps, step, place, back)
        return result[: rows // LANES].reshape(rows), a[0, -1]

    def body(embeddings, cluster_id, cluster_rank):
        share = embeddings.shape[0] // ngrp
        usual = ceil_to(share + 1, 16)
        most = ceil_to(2 * share + 1, 16)
        result, over = attempt(usual, True, embeddings, cluster_id, cluster_rank)

        def again():
            return attempt(most, False, embeddings, cluster_id, cluster_rank)[0]

        return lax.cond(over > 0.5, again, lambda: result)

    placed = (P(AXES, None), P(AXES), P(AXES))
    return jax.shard_map(body, mesh=mesh, in_specs=placed, out_specs=P(AXES), check_vma=False)
```

```python
import functools

import jax
import jax.numpy as jnp
from jax import lax
from jax.experimental import pallas as pl
from jax.experimental.pallas import tpu as pltpu
from jax.sharding import PartitionSpec as P

AXES = ("grp", "sub")
LANES = 128
RADIX = 128
EMPTY = 255.0
VMEM = 16 * 1024 * 1024


def ceil_to(value, unit):
    return -(-value // unit) * unit


def nt_dot(left, right):
    return lax.dot_general(
        left, right, (((1,), (1,)), ((), ())), preferred_element_type=jnp.float32
    )


def steps(pieces):
    bits = (pieces - 1).bit_length()
    return [sum((p >> i & 1) << (bits - 1 - i) for i in range(bits)) for p in range(pieces)]


def in_place(array):
    return pltpu.with_memory_space_constraint(array, pltpu.VMEM)


def after(blocks, earlier):
    if not earlier:
        return blocks
    held = [in_place(x) for x in blocks]
    return list(pl.pallas_call(
        lambda *refs: None,
        out_shape=[pltpu.VMEM(x.shape, x.dtype) for x in blocks],
        in_specs=[pl.BlockSpec(memory_space=pltpu.VMEM)] * len(blocks)
        + [pl.BlockSpec(memory_space=pl.ANY)] * len(earlier),
        out_specs=[pl.BlockSpec(memory_space=pltpu.VMEM)] * len(blocks),
        input_output_aliases={i: i for i in range(len(blocks))},
        compiler_params=pltpu.CompilerParams(vmem_limit_bytes=VMEM),
        name="after",
    )(*held, *earlier))


def sizes(pieces, cap):
    return [cap] * pieces


def starts_of(counts):
    return [sum(counts[:i]) for i in range(len(counts))]


def flat(ref):
    return jnp.concatenate([ref[b : b + 1, :] for b in range(ref.shape[0])], axis=1)


def fill(first, caps, flagged, outs, emb, sorting, pick, raw, copies=()):
    rows, width = emb.shape
    target = sorting[0:1, :].astype(jnp.int32)
    digits = jnp.concatenate([sorting[...], jnp.zeros((8, rows), jnp.float32)], axis=0)
    digits = digits.astype(jnp.bfloat16)
    notes = []
    starts = starts_of(caps)
    for i, cap in enumerate(caps):
        lanes_per = ceil_to(cap, LANES)
        slots = lax.broadcasted_iota(jnp.int32, (lanes_per, rows), 0) + (first + i) * 1024
        found = jnp.where(slots == target, 1.0, 0.0).astype(jnp.bfloat16)
        pick[starts[i] : starts[i] + cap, :] = found[:cap]
        ranks = nt_dot(digits, found)
        parts = [jnp.where(ranks[3:4, :] > 0.5, ranks[1:2, :], EMPTY), ranks[2:3, :]]
        if flagged:
            parts.append(jnp.broadcast_to(sorting[4:5, :LANES], (1, LANES)))
        used = 2 * lanes_per + (LANES if flagged else 0)
        if used < width:
            parts.append(jnp.zeros((1, width - used), jnp.float32))
        notes.append(jnp.concatenate(parts, axis=1))
    for copy in copies:
        copy.wait()
    for at in range(0, width, 256):
        lanes = slice(at, at + 256)
        raw[:, lanes] = jnp.dot(pick[...], emb[:, lanes], preferred_element_type=jnp.float32)
    last = lax.broadcasted_iota(jnp.int32, (16, 1), 0) == 15
    for i, (cap, out) in enumerate(zip(caps, outs)):
        wide = raw[starts[i] : starts[i] + cap, :]
        scale = lax.rsqrt(jnp.sum(wide * wide, axis=1, keepdims=True) + 1e-06)
        unit = wide * scale
        out[: cap - 16, :] = unit[: cap - 16].astype(jnp.bfloat16)
        out[cap - 16 :, :] = jnp.where(last, notes[i], unit[cap - 16 :]).astype(jnp.bfloat16)


def sort_kernel(pieces, low, caps, flagged, emb, cid, rank, *refs):
    out, held, sorting, place, pick, raw, slot_ref, sem = refs
    rows, width = held.shape
    parts = 4
    share = rows // parts
    copies = []
    for i in range(parts):
        at = pl.ds(i * share, share)
        copy = pltpu.make_async_copy(emb.at[at, :], held.at[at, :], sem.at[i])
        copy.start()
        copies.append(copy)

    plane = lax.axis_index("sub") // low
    step = flat(cid) ^ plane
    piece = jnp.zeros(step.shape, jnp.int32)
    for p, s in enumerate(steps(pieces)):
        piece = jnp.where(step == s, p, piece)
    which = lax.broadcasted_iota(jnp.int32, (16, LANES), 0)
    upper = (
        lax.broadcasted_iota(jnp.int32, (LANES, LANES), 0)
        < lax.broadcasted_iota(jnp.int32, (LANES, LANES), 1)
    ).astype(jnp.bfloat16)
    before = jnp.zeros((16, 1), jnp.float32)
    for b in range(rows // LANES):
        lanes = slice(b * LANES, (b + 1) * LANES)
        member = piece[:, lanes] == which
        ones = member.astype(jnp.float32)
        prefix = jnp.dot(ones.astype(jnp.bfloat16), upper, preferred_element_type=jnp.float32)
        slot = jnp.sum(jnp.where(member, prefix + before, 0.0), axis=0, keepdims=True)
        slot_ref[:, lanes] = slot.astype(jnp.int32)
        before = before + jnp.sum(ones, axis=1, keepdims=True)
    slot = slot_ref[...]
    lane_starts = starts_of([ceil_to(c, LANES) for c in caps])
    spot = slot
    for p in range(1, len(caps)):
        spot = spot + jnp.where(piece == p, lane_starts[p], 0)
    place[...] = jnp.zeros(place.shape, jnp.int32)
    for b in range(rows // LANES):
        place[b : b + 1, :] = spot[:, b * LANES : (b + 1) * LANES]
    full = (jnp.max(before, axis=0, keepdims=True) > caps[0] - 1).astype(jnp.float32)
    r = flat(rank)
    sorting[0:1, :] = (piece * 1024 + slot).astype(jnp.float32)
    sorting[1:2, :] = (r // RADIX).astype(jnp.float32)
    sorting[2:3, :] = (r % RADIX).astype(jnp.float32)
    sorting[3:4, :] = jnp.ones((1, rows), jnp.float32)
    sorting[4:5, :] = jnp.broadcast_to(full, (1, rows))
    sorting[5:8, :] = jnp.zeros((3, rows), jnp.float32)

    fill(1, caps[1:2], flagged, [out], held, sorting, pick, raw, copies)


def fill_kernel(first, caps, flagged, emb, sorting, *refs):
    fill(first, caps, flagged, refs[:-2], emb, sorting, refs[-2], refs[-1])


def dispatch(pieces, low, caps, flagged, emb, cid, rank):
    rows, width = emb.shape
    bf16 = jnp.bfloat16
    in_vmem = pl.BlockSpec(memory_space=pltpu.VMEM)
    one, held, sorting, place = pl.pallas_call(
        functools.partial(sort_kernel, pieces, low, caps, flagged),
        out_shape=[
            pltpu.VMEM((caps[1], width), bf16),
            pltpu.VMEM((rows, width), bf16),
            pltpu.VMEM((8, rows), jnp.float32),
            pltpu.VMEM((8, LANES), jnp.int32),
        ],
        in_specs=[pl.BlockSpec(memory_space=pl.ANY), in_vmem, in_vmem],
        out_specs=[in_vmem] * 4,
        scratch_shapes=[
            pltpu.VMEM((caps[1], rows), bf16),
            pltpu.VMEM((caps[1], width), jnp.float32),
            pltpu.VMEM((1, rows), jnp.int32),
            pltpu.SemaphoreType.DMA((4,)),
        ],
        compiler_params=pltpu.CompilerParams(vmem_limit_bytes=VMEM),
        name="sort",
    )(emb, cid.reshape(rows // LANES, LANES), rank.reshape(rows // LANES, LANES))

    def more(first, stop):
        return list(
            pl.pallas_call(
                functools.partial(fill_kernel, first, caps[first:stop], flagged),
                out_shape=[pltpu.VMEM((cap, width), bf16) for cap in caps[first:stop]],
                in_specs=[in_vmem, in_vmem],
                out_specs=[in_vmem] * (stop - first),
                scratch_shapes=[
                    pltpu.VMEM((sum(caps[first:stop]), rows), bf16),
                    pltpu.VMEM((sum(caps[first:stop]), width), jnp.float32),
                ],
                compiler_params=pltpu.CompilerParams(vmem_limit_bytes=VMEM),
                name="fill" + str(first),
            )(in_place(held), in_place(sorting))
        )

    return more(0, 1) + [one] + more(2, len(caps)), place


def stage_kernel(p, part, caps, groups, flagged, *refs):
    new = {"all": range(groups), "home": range(2), "away": range(2, groups)}[part]
    blocks, refs = refs[: len(new)], refs[len(new) :]
    if p or part == "away":
        refs = refs[3:]
    store, limits, best, token, refs = *refs[:4], refs[4:]
    *ends, keys, cols, sem = refs
    token[...] = jnp.zeros(token.shape, jnp.float32)
    cap = caps[p]
    mine, near = 1, groups - 1
    lanes = [ceil_to(c, LANES) for c in caps]
    base = groups * starts_of(caps)[p]
    lane_base = [groups * s for s in starts_of(lanes)]
    wide = lanes[p]

    copies = []
    for g, block in zip(new, blocks):
        copy = pltpu.make_async_copy(block, store.at[pl.ds(base + g * cap, cap), :], sem.at[g])
        copy.start()
        copies.append(copy)

    lane = lax.broadcasted_iota(jnp.int32, (1, wide), 1)
    square = lax.broadcasted_iota(jnp.int32, (cap, wide), 0) == lax.broadcasted_iota(
        jnp.int32, (cap, wide), 1
    )
    flag = jnp.zeros((1, LANES), jnp.float32)
    if p == 0 and part != "away":
        best[...] = jnp.full(best.shape, -1.0, jnp.float32)
    cols[...] = jnp.full(cols.shape, -1.0, jnp.float32)
    for g, block in zip(new, blocks):
        note = block[cap - 16 :, :].astype(jnp.float32)[15:16, :]
        ranks = note[:, :wide] * RADIX + note[:, wide : 2 * wide]
        ranks = jnp.where(lane < cap - 1, ranks, EMPTY * RADIX)
        if flagged:
            flag = jnp.maximum(flag, note[:, 2 * wide : 2 * wide + LANES])
        at = lane_base[p] + g * wide
        limits[:, at : at + wide] = jnp.broadcast_to(ranks, (8, wide))
        column = jnp.sum(jnp.where(square, ranks, 0.0), axis=1, keepdims=True)
        keys[g * cap : (g + 1) * cap, :] = jnp.broadcast_to(column, (cap, LANES))
    if flagged:
        at = best.shape[1] - LANES
        best[:, at:] = jnp.maximum(best[:, at:], jnp.broadcast_to(flag, (8, LANES)))
    for copy in copies:
        copy.wait()

    def product(first, at, count, g, runs):
        if not runs:
            return
        query = store[pl.ds(first, count), :]
        limit = limits[0:1, pl.ds(at, count)]
        top = best[:, pl.ds(at, count)]
        for start, size, low, high in runs:
            start, size, low, high = start * cap, size * cap, low * cap, high * cap
            sims = nt_dot(store[base + start : base + start + size, :], query)
            kr = jnp.concatenate([keys[start : start + size, :]] * (count // LANES), axis=1)
            earlier = kr < limit
            if g:
                ahead = jnp.where(earlier, sims, -1.0)
                top = jnp.maximum(top, jnp.max(ahead.reshape(size // 8, 8, count), axis=0))
            if low < high:
                behind = jnp.where(earlier, -1.0, sims)[low - start : high - start]
                fold = cols[low:high, :]
                for k in range(0, count, LANES):
                    fold = jnp.maximum(fold, behind[:, k : k + LANES])
                cols[low:high, :] = fold
        if g:
            best[:, pl.ds(at, count)] = top

    def partners(g, alone):
        just_mine = [] if alone else [(mine, 1, mine, 2)]
        if part == "home":
            if g == mine:
                return [(0, 2, 1, 1 if alone else 2)]
            return just_mine
        if part == "away":
            if g == mine:
                return [(2, groups - 2, 2, groups)]
            if g == near:
                return [(2, near - 2, 2, near)]
            return [] if alone or g == 0 else [(near, 1, near, groups)]
        if g == mine:
            return [(0, near, 2, near)] if alone else [(0, groups, 1, groups)]
        if g == near:
            return [(mine, near - 1, mine, near)]
        if alone or g == 0:
            return just_mine
        return [(mine, 1, mine, 2), (near, 1, near, groups)]

    def old(i):
        for g in range(groups):
            at = (i * groups + g) * wide
            first = (i * groups + g) * cap
            if part != "away":
                first, at = pl.multiple_of(first, 16), pl.multiple_of(at, LANES)
            product(first, at, wide, g, partners(g, False))

    if part == "away":
        for i in range(p):
            old(i)
    elif p:
        pl.loop(0, p)(old)

    for g in range(groups):
        product(base + g * cap, lane_base[p] + g * wide, wide, g, partners(g, True))

    for g in new:
        if g:
            at = lane_base[p] + g * wide
            column = jnp.max(cols[g * cap : (g + 1) * cap, :], axis=1, keepdims=True)
            turned = jnp.max(jnp.where(square, column, -1.0), axis=0, keepdims=True)
            best[:, at : at + wide] = jnp.maximum(best[:, at : at + wide], turned)

    for g, out in enumerate(ends, start=1):
        for q, start in enumerate(starts_of(lanes)):
            at = lane_base[q] + g * lanes[q]
            row = jnp.max(best[:, at : at + lanes[q]], axis=0, keepdims=True)
            out[:, start : start + lanes[q]] = row
        out[:, sum(lanes) :] = best[0:1, best.shape[1] - LANES :]


def stage(p, part, caps, groups, flagged, blocks, carried):
    width = blocks[0].shape[1]
    lanes = sum(ceil_to(c, LANES) for c in caps)
    f32 = jnp.float32
    in_vmem = pl.BlockSpec(memory_space=pltpu.VMEM)
    kept = [
        pltpu.VMEM((groups * sum(caps) + LANES, width), jnp.bfloat16),
        pltpu.VMEM((8, groups * lanes), f32),
        pltpu.VMEM((8, groups * lanes + LANES), f32),
        jax.ShapeDtypeStruct((8, LANES), f32),
    ]
    ends = [jax.ShapeDtypeStruct((1, lanes + LANES), f32)] * (groups - 1)
    if p < len(caps) - 1 or part == "home":
        ends = []
    got = pl.pallas_call(
        functools.partial(stage_kernel, p, part, caps, groups, flagged),
        out_shape=kept + ends,
        in_specs=[in_vmem] * (len(blocks) + len(carried)),
        out_specs=[in_vmem] * (4 + len(ends)),
        scratch_shapes=[
            pltpu.VMEM((groups * caps[p], LANES), f32),
            pltpu.VMEM((groups * caps[p], LANES), f32),
            pltpu.SemaphoreType.DMA((groups,)),
        ],
        input_output_aliases={len(blocks) + i: i for i in range(len(carried))},
        cost_estimate=pl.CostEstimate(flops=0, bytes_accessed=0, transcendentals=0),
        compiler_params=pltpu.CompilerParams(vmem_limit_bytes=VMEM),
        name="stage" + str(p) + part,
    )(*[in_place(x) for x in blocks], *[in_place(x) for x in carried])
    return got[:3], got[3], got[4:]


def collect_kernel(lanes, step, place, *refs):
    rows, out = refs[:-1], refs[-1]
    where = place[...]
    result = jnp.zeros((8, LANES), jnp.float32)
    for q, start in enumerate(starts_of(lanes)):
        for first in range(start, start + lanes[q], LANES):
            back = jnp.broadcast_to(rows[step[q]][:, first : first + LANES], (8, LANES))
            inside = where - first
            hit = (inside >= 0) & (inside < LANES)
            taken = jnp.take_along_axis(back, jnp.where(hit, inside, 0), axis=1)
            result = jnp.where(hit, taken, result)
    out[...] = result


def collect(caps, step, place, rows):
    lanes = [ceil_to(c, LANES) for c in caps]
    return pl.pallas_call(
        functools.partial(collect_kernel, lanes, step),
        out_shape=jax.ShapeDtypeStruct((8, LANES), jnp.float32),
        in_specs=[pl.BlockSpec(memory_space=pltpu.VMEM)] * (1 + len(rows)),
        name="collect",
    )(*[in_place(x) for x in [place] + rows])


def solution(mesh):
    ngrp, nsub = mesh.shape["grp"], mesh.shape["sub"]
    low = nsub // ngrp
    pieces = ngrp
    chips = ngrp // 2

    def send(block, target):
        route = []
        for g in range(ngrp):
            for s in range(nsub):
                chip, core, plane, small = target(g // 2, g % 2, s // low, s % low)
                route.append((g * nsub + s, (chip * 2 + core) * nsub + plane * low + small))
        return lax.ppermute(block, AXES, route)

    def to_plane(block, s):
        return send(block, lambda x, c, z, y: (x, c, z ^ s, y))

    def to_twin(block):
        return send(block, lambda x, c, z, y: (x, 1 - c, z, y))

    def bit(x, j):
        return (x // (j & -j)) % 2

    def to_near(block):
        return send(block, lambda x, c, z, y: (x, c ^ (1 - y), z, 1 - y))

    def from_near(block):
        return send(block, lambda x, c, z, y: (x, c ^ y, z, 1 - y))

    def to_cross(block, j):
        return send(block, lambda x, c, z, y: (x ^ j, c ^ y ^ bit(x ^ j, j), z, y))

    def from_cross(block, j):
        return send(block, lambda x, c, z, y: (x ^ j, c ^ y ^ bit(x, j), z, y))

    def attempt(cap, flagged, embeddings, cluster_id, cluster_rank):
        rows = embeddings.shape[0]
        caps = sizes(pieces, cap)
        count = len(caps)
        step = steps(pieces)
        own, place = dispatch(pieces, low, caps, flagged, embeddings, cluster_id, cluster_rank)
        moved = [own[0]] + [None] * (count - 1)

        def leave(q, earlier):
            moved[q] = to_plane(after([own[q]], earlier)[0], step[q])

        leave(1, [])
        links, carried, tokens = [], [], []
        for p in range(count):
            earlier = links[p - 2] if p >= 2 else []
            if p > 1:
                earlier = earlier + [tokens[p - 1 - 1]]
            (mine,) = after([moved[p]], earlier)
            twin = to_twin(mine)
            if p == 0:
                (mine,) = after([mine], [twin])
            cross = [to_cross(mine, j) for j in range(1, chips)]
            near = to_near(mine)
            links.append(cross + [near, twin])
            groups = 3 + len(cross)
            home, away = [twin, mine], cross + [near]
            if p in (count - 1,):
                carried, token, ends = stage(p, "home", caps, groups, flagged, home, carried)
                if p == 0:
                    for q in range(2, pieces):
                        leave(q, [token] if q == 2 else [])
                carried, token, ends = stage(p, "away", caps, groups, flagged, away, carried)
            else:
                if p == 0:
                    for q in range(2, pieces):
                        leave(q, [twin] if q == 2 else [])
                carried, token, ends = stage(p, "all", caps, groups, flagged, home + away, carried)
            tokens.append(token)
        a = jnp.maximum(ends[0], from_near(ends[-1]))
        for j in range(1, chips):
            a = jnp.maximum(a, from_cross(ends[j], j))
        back = [a] + [to_plane(a, s) for s in range(1, pieces)]
        result = collect(caps, step, place, back)
        return result[: rows // LANES].reshape(rows), a[0, -1]

    def body(embeddings, cluster_id, cluster_rank):
        share = embeddings.shape[0] // ngrp
        usual = ceil_to(share + 1, 16)
        most = ceil_to(2 * share + 1, 16)
        result, over = attempt(usual, True, embeddings, cluster_id, cluster_rank)

        def again():
            return attempt(most, False, embeddings, cluster_id, cluster_rank)[0]

        return lax.cond(over > 0.5, again, lambda: result)

    placed = (P(AXES, None), P(AXES), P(AXES))
    return jax.shard_map(body, mesh=mesh, in_specs=placed, out_specs=P(AXES), check_vma=False)
```
